256 devices in a mesh: reg: 32 (over z, x_lo, core), glob: 4 (over y), cpl: 2 (over x_hi).
Axes of the slice: x: 4 (x_hi: 2, x_lo: 2; x = x_hi * 2 + x_lo), y: 4, z: 8, core: 2. Of those that a mesh axis runs over, the one named last changes fastest.
Arguments:
- saved_input: bfloat16 [2, 172, 512, 512], P('cpl', None, 'reg', 'glob'), may hold values from -6 to 6
- pre_act: bfloat16 [2, 128, 512, 512], P('cpl', None, 'reg', 'glob'), may hold values from -8 to 8
- cotangent: bfloat16 [2, 128, 512, 512], P('cpl', None, 'reg', 'glob'), may hold values from -6 to 6
- conv_weight: bfloat16 [9, 172, 128], replicated, may hold values from -0.15625 to 0.15625
- interp: bfloat16 [4, 512, 128, 128], P('glob', 'reg'), may hold values from -0.5 to 0.5
- targets: int32 [4, 512], P('glob', 'reg'), may hold values from 0 to 255, as said below
- noise_index: int32 [2], P('cpl'), may hold values from 0 to 17
Outputs:
- input_grad: bfloat16 [2, 99, 512, 512], P('cpl', None, 'reg', 'glob')
- weight_grad: float32 [9, 172, 128], replicated
- bias_grad: float32 [128], replicated
- global_grad: float32 [256, 73, 128], P(('reg', 'glob'))
The draws below stay inside these ranges and needn't reach their ends.
Inputs may be any that keep to these rules, and one draw needn't show every extreme that they name: `targets`: with h = ((r // 16) * 4 + g) * 2, row block (g, r) reads a global block h - 1 to h + 2 modulo 256, except that the second of every 16 rows reads block h + 256 // 2 modulo 256; the first of every 16 rows reads h - 1 and the last reads h + 2.
All inputs are finite; a program needn't handle non-finite values.
Results may differ from the reference program's by a relative error of at most 0.0054.
Values may be sent and summed in bfloat16 or wider, within the bound.
A program may use at most 128 MiB of HBM per device.

```python
import math
import jax
import jax.numpy as jnp
from jax import lax

CH = 128
CR = 99
CG = 73
TC = 128
GPTS = 128
GB_DEV = 2
NOISE_LEVELS = 18
TR = 16
CIN = 172
ROWS = 512
COLS = 512
NGB = 256
SAMPLES = 2
N_GLOB = 4


def draw_targets(key, part):
    key = jax.random.fold_in(key, 7)
    jitter = jax.random.randint(key, (N_GLOB, ROWS), -1, GB_DEV + 1)
    row_ids = jnp.arange(ROWS, dtype=jnp.int32)[None, :]
    col_ids = jnp.arange(N_GLOB, dtype=jnp.int32)[:, None]
    within = row_ids % TR
    jitter = jnp.where(within == 0, -1, jnp.where(within == TR - 1, GB_DEV, jnp.where(within == 1, NGB // 2, jitter)))
    home = (row_ids // TR * N_GLOB + col_ids) * GB_DEV
    return ((home + jitter + NGB) % NGB).astype(jnp.int32)


def levels(stream_key, extent, shards, low, high):
    level = 1.0
    for position, shards_of in shards:
        steps = jax.random.uniform(jax.random.fold_in(jax.random.fold_in(stream_key, 6), position), (shards_of,), jnp.float32, low / len(shards), high / len(shards))
        level = level * jnp.repeat(jnp.exp(steps), extent[position] // shards_of).reshape((-1,) + (1,) * (len(extent) - 1 - position))
    return level


def noise(key, shape, deviation, most, cuts=(), kind=jnp.bfloat16):
    drawn = deviation * jax.random.normal(key, shape, jnp.float32)
    if cuts:
        drawn = drawn * levels(key, shape, cuts, -0.22, 0.18)
    return jnp.clip(drawn, -most, most).astype(kind)


def setup_inputs(seed: int = 0) -> dict:
    keys = jax.random.split(jax.random.key(seed), 8)
    return {
        "saved_input": noise(keys[0], (SAMPLES, CIN, ROWS, COLS), 1.0, 6.0, ((0, 2), (2, 32), (3, 4))),
        "pre_act": noise(keys[1], (SAMPLES, CH, ROWS, COLS), 1.5, 8.0, ((0, 2), (2, 32), (3, 4))),
        "cotangent": noise(keys[2], (SAMPLES, CH, ROWS, COLS), 1.0, 6.0, ((0, 2), (2, 32), (3, 4))),
        "conv_weight": noise(keys[3], (9, CIN, CH), (9 * CIN) ** -0.5, 0.15625),
        "interp": noise(keys[4], (N_GLOB, ROWS, TC, GPTS), GPTS ** -0.5, 0.5, ((0, 4), (1, 32))),
        "targets": draw_targets(jax.random.fold_in(keys[7], 71), 0),
        "noise_index": jax.random.randint(keys[6], (SAMPLES,), 0, NOISE_LEVELS).astype(jnp.int32),
    }


def noise_scale(index):
    frac = index.astype(jnp.float32) / (NOISE_LEVELS - 1)
    sigma = jnp.exp(jnp.log(2.0) + frac * (jnp.log(0.05) - jnp.log(2.0)))
    return 1.0 / jnp.sqrt(sigma * sigma + 0.25)

def reference(saved_input, pre_act, cotangent, conv_weight, interp, targets, noise_index):
    scale_norm = 1.0 / math.sqrt(ROWS * COLS * SAMPLES)
    weight_sum = jnp.zeros((9, CIN, CH), jnp.float32)
    bias_sum = jnp.zeros((CH,), jnp.float32)
    global_sum = jnp.zeros((NGB, CG * GPTS), jnp.float32)
    interp_wide = interp.astype(jnp.float32)
    flat_targets = targets.reshape(N_GLOB * ROWS).astype(jnp.int32)
    grads = []
    for sample in range(SAMPLES):
        pre = pre_act[sample].astype(jnp.float32)
        sig = jax.nn.sigmoid(pre)
        dz32 = cotangent[sample].astype(jnp.float32) * sig * (1.0 + pre * (1.0 - sig))
        bias_sum = bias_sum + lax.optimization_barrier(jnp.sum(dz32, axis=(1, 2)))
        padded = jnp.pad(dz32.astype(jnp.bfloat16), ((0, 0), (1, 1), (1, 1)))
        inputs = saved_input[sample].reshape(CIN, ROWS * COLS)
        back = jnp.zeros((CIN, ROWS * COLS), jnp.float32)
        for offset in range(9):
            shift_row = offset // 3 - 1
            shift_col = offset % 3 - 1
            shifted = padded[:, 1 - shift_row:1 - shift_row + ROWS, 1 - shift_col:1 - shift_col + COLS].reshape(CH, ROWS * COLS)
            back = back + jnp.dot(conv_weight[offset], shifted, preferred_element_type=jnp.float32)
            term = lax.dot_general(inputs, shifted, (((1,), (1,)), ((), ())), preferred_element_type=jnp.float32)
            weight_sum = weight_sum.at[offset].add(term)
        grads.append((noise_scale(noise_index[sample]) * back[:CR]).reshape(CR, ROWS, COLS).astype(jnp.bfloat16))
        rounded = lax.optimization_barrier(back[CR:].astype(jnp.bfloat16))
        cond = rounded.astype(jnp.float32).reshape(CG, ROWS, N_GLOB, TC)
        blocks = jnp.transpose(cond, (2, 1, 0, 3))
        contrib = jnp.einsum('grct,grtj->grcj', blocks, interp_wide, precision=lax.Precision.HIGHEST)
        global_sum = global_sum + jax.ops.segment_sum(contrib.reshape(N_GLOB * ROWS, CG * GPTS), flat_targets, num_segments=NGB)
    input_grad = jnp.stack(grads, 0)
    return (input_grad, weight_sum * scale_norm, bias_sum * scale_norm, global_sum.reshape(NGB, CG, GPTS))
```

```python
import math

import jax
import jax.numpy as jnp
from jax import lax
from jax.experimental import pallas as pl
from jax.experimental.pallas import tpu as pltpu
from jax.sharding import PartitionSpec as P

CH = 128
CR = 99
CG = 73
CIN = 172
CPAD = 176
HALF = 88
TR = 16
TC = 128
NGB = 256
NOISE_LEVELS = 18
PIECE = 56
PIECE_B = 64
ROWS_HALF = 9 * HALF
ROWS_ALL = 16 * PIECE
TOP = 8
PITCH = TOP + TC + 8
BLK = 80
SCALE_NORM = 1.0 / math.sqrt(512 * 512 * 2)
MESH = pl.DeviceIdType.MESH
F32 = jnp.float32
BF16 = jnp.bfloat16


def kernel(
    saved_hbm, pre_hbm, cot_hbm, w_hbm, interp_hbm, targets_ref, noise_ref,
    igrad_hbm, wgrad_ref, bgrad_ref, ggrad_ref,
    saved_v, pre_v, cot_v, w_v, interp_v,
    d32, s32, p32, dzc, smat, wcat, colbuf, colrecv, corner,
    awh, crecv, acc, xrecv, zbuf, fbuf, gbuf,
    bk32, cmask, glob_out, glob_recv, own, cplrecv, ig_v,
    in_sem, halo_ss, halo_rs, core_ss, core_rs, xy_ss, xy_rs, z_ss, z_rs,
    ag_ss, ag_rs, fw_ss, fw_rs, gl_ss, gl_rs, out_sem,
):
    reg = lax.axis_index("reg")
    glob = lax.axis_index("glob")
    cpl = lax.axis_index("cpl")
    z = reg // 4
    x_lo = (reg // 2) % 2
    core = reg % 2
    x = cpl * 2 + x_lo
    y = glob
    q = x * 4 + y

    def at(x_, y_, z_, core_):
        return {"reg": z_ * 4 + (x_ % 2) * 2 + core_, "glob": y_, "cpl": x_ // 2}

    def plane(d):
        return (x + d // 4) % 4, (y + d % 4) % 4

    def plane_dev(d):
        px, py = plane(d)
        return at(px, py, z, core)

    def z_dev(d):
        return at(x, y, (z + d) % 8, core)

    def halo_dev(dr, dg):
        return {"reg": (reg + dr + 32) % 32, "glob": (glob + dg + 4) % 4, "cpl": cpl}

    def flat_dev(step):
        flat = (reg * 4 + glob + step + 128) % 128
        return {"reg": flat // 4, "glob": flat % 4, "cpl": cpl}

    sibling = at(x, y, z, 1 - core)
    other = {"reg": reg, "glob": glob, "cpl": 1 - cpl}

    loads = [
        pltpu.make_async_copy(src, dst, in_sem.at[n])
        for n, (src, dst) in enumerate((
            (pre_hbm.at[0], pre_v),
            (cot_hbm.at[0], cot_v),
            (saved_hbm.at[0], saved_v),
            (w_hbm, w_v),
            (interp_hbm.at[0], interp_v),
        ))
    ]
    for load in loads:
        load.start()

    barrier = pltpu.get_barrier_semaphore()

    def greet(device):
        pl.semaphore_signal(barrier, inc=1, device_id=device, device_id_type=MESH)

    halo_steps = [(dr, dg) for dr in (-1, 0, 1) for dg in (-1, 0, 1) if dr or dg]
    for dr, dg in halo_steps:
        greet(halo_dev(dr, dg))
    for step in (-1, 1, 64):
        greet(flat_dev(step))
    greet(other)
    greet(sibling)
    lax.fori_loop(1, 16, lambda d, c: (greet(plane_dev(d)), c)[1], 0)
    lax.fori_loop(1, 8, lambda d, c: (greet(z_dev(d)), c)[1], 0)

    s32[CIN * TR :, :] = jnp.zeros((CPAD * TR - CIN * TR, TC), F32)
    wcat[:, CPAD - 16 :, :] = jnp.zeros((3, 16, 3 * CH), BF16)
    acc[ROWS_HALF:, :] = jnp.zeros((ROWS_ALL - ROWS_HALF, CH), F32)
    bk32[:, CPAD:, :] = jnp.zeros((TR, 8, TC), F32)

    loads[0].wait()
    loads[1].wait()

    def silu_step(n, carry):
        pre = pre_v[pl.ds(n * 8, 8)].astype(F32)
        cot = cot_v[pl.ds(n * 8, 8)].astype(F32)
        sig = 0.5 * jnp.tanh(0.5 * pre) + 0.5
        dz = cot * sig * (1.0 + pre * (1.0 - sig))
        d32[pl.ds(pl.multiple_of(n * 8 * TR, 128), 8 * TR), :] = dz.reshape(8 * TR, TC)
        return carry

    lax.fori_loop(0, CH // 8, silu_step, 0)

    def turn(i):
        tile = jnp.transpose(d32[pl.ds(i, CH, stride=TR), :], (1, 0))
        p32[i + 1, TOP : TOP + TC, :] = tile
        colbuf[0, i : i + 1, :] = tile[:1]
        colbuf[1, i : i + 1, :] = tile[TC - 1 :]
        return tile

    total = jnp.zeros((TC, CH), F32)
    for i in range(TR):
        total = total + turn(i)
    bias = jnp.sum(total, axis=0, keepdims=True)

    pl.semaphore_wait(barrier, 8 + 3 + 1 + 1 + 15 + 7)

    halo = []
    for n, (dr, dg) in enumerate(halo_steps):
        row = TR if dr > 0 else 1
        if dg == 0:
            src = p32.at[row, pl.ds(TOP, TC)]
            dst = p32.at[0 if dr > 0 else TR + 1, pl.ds(TOP, TC)]
        elif dr == 0:
            src = colbuf.at[1 if dg > 0 else 0]
            dst = colrecv.at[0 if dg > 0 else 1]
        else:
            src = p32.at[row, pl.ds(TOP + TC - 8 if dg > 0 else TOP, 8)]
            dst = corner.at[0 if dr > 0 else 1, 0 if dg > 0 else 1]
        copy = pltpu.make_async_remote_copy(
            src, dst, halo_ss.at[n], halo_rs.at[n],
            device_id=halo_dev(dr, dg), device_id_type=MESH,
        )
        copy.start()
        halo.append(copy)

    loads[2].wait()

    def saved_step(n, carry):
        part = saved_v[pl.ds(n * 4, 4)].astype(F32)
        s32[pl.ds(pl.multiple_of(n * 4 * TR, 64), 4 * TR), :] = part.reshape(4 * TR, TC)
        return carry

    lax.fori_loop(0, CIN // 4, saved_step, 0)
    for i in range(TR):
        smat[:, i * TC : (i + 1) * TC] = s32[pl.ds(i, CPAD, stride=TR), :].astype(BF16)

    def shift_rows(i):
        for bi in range(3):
            dzc[pl.ds(pl.multiple_of(i * TC, TC), TC), bi * CH : (bi + 1) * CH] = p32[
                i, TOP + 1 - bi : TOP + 1 - bi + TC, :
            ].astype(BF16)

    loads[3].wait()
    for a in range(3):
        for bi in range(3):
            wcat[a, :CIN, bi * CH : (bi + 1) * CH] = w_v[3 * a + bi]

    for copy in halo:
        copy.wait_recv()
    up = (reg > 0).astype(F32)
    down = (reg < 31).astype(F32)
    left = (glob > 0).astype(F32)
    right = (glob < 3).astype(F32)
    p32[0, TOP : TOP + TC, :] = p32[0, TOP : TOP + TC, :] * up
    p32[TR + 1, TOP : TOP + TC, :] = p32[TR + 1, TOP : TOP + TC, :] * down
    for i in range(TR):
        p32[i + 1, TOP - 1 : TOP, :] = colrecv[0, i : i + 1, :] * left
        p32[i + 1, TOP + TC : TOP + TC + 1, :] = colrecv[1, i : i + 1, :] * right
    p32[0, TOP - 1 : TOP, :] = corner[0, 0, 7:8, :] * (up * left)
    p32[0, TOP + TC : TOP + TC + 1, :] = corner[0, 1, 0:1, :] * (up * right)
    p32[TR + 1, TOP - 1 : TOP, :] = corner[1, 0, 7:8, :] * (down * left)
    p32[TR + 1, TOP + TC : TOP + TC + 1, :] = corner[1, 1, 0:1, :] * (down * right)

    lax.fori_loop(0, TR + 2, lambda i, c: (shift_rows(i), c)[1], 0)

    core_copies = []
    for a in range(3):
        term = jnp.dot(
            smat[...], dzc[(2 - a) * TC : (2 - a) * TC + TR * TC, :],
            preferred_element_type=F32,
        )
        for bi in range(3):
            k = 3 * a + bi
            for h in range(2):
                awh[h, k * HALF : (k + 1) * HALF, :] = term[
                    h * HALF : (h + 1) * HALF, bi * CH : (bi + 1) * CH
                ]
        if a == 0:
            awh[1, CIN - HALF : CIN - HALF + 1, :] = bias
        rows = pl.ds(3 * a * HALF, 3 * HALF)
        copy = pltpu.make_async_remote_copy(
            awh.at[1 - core, rows], crecv.at[rows], core_ss.at[a], core_rs.at[a],
            device_id=sibling, device_id_type=MESH,
        )
        copy.start()
        core_copies.append(copy)
    for a in range(3):
        core_copies[a].wait_recv()
        rows = pl.ds(3 * a * HALF, 3 * HALF)
        acc[rows, :] = awh[core, rows, :] + crecv[rows, :]

    def xy_copy(d):
        px, py = plane(d)
        return pltpu.make_async_remote_copy(
            acc.at[pl.ds(pl.multiple_of((px * 4 + py) * PIECE, 8), PIECE)],
            xrecv.at[d], xy_ss.at[d], xy_rs.at[d],
            device_id=at(px, py, z, core), device_id_type=MESH,
        )

    lax.fori_loop(0, 15, lambda n, c: (xy_copy(15 - n).start(), c)[1], 0)

    level = jnp.full((1, TC), noise_ref[0], jnp.int32).astype(F32) / (NOISE_LEVELS - 1)
    sigma = jnp.exp(math.log(2.0) + level * (math.log(0.05) - math.log(2.0)))
    scale = 1.0 / jnp.sqrt(sigma * sigma + 0.25)

    def back_step(n, carry):
        back = jnp.zeros((CPAD, 2 * TC), F32)
        for a in range(3):
            start = pl.multiple_of((2 * n + 2 - a) * TC, TC)
            back = back + lax.dot_general(
                wcat[a], dzc[pl.ds(start, 2 * TC), :], (((1,), (1,)), ((), ())),
                preferred_element_type=F32,
            )
        for half in range(2):
            part = back[:, half * TC : (half + 1) * TC]
            bk32[2 * n + half, :CPAD, :] = part
            d32[pl.ds(2 * n + half, CR, stride=TR), :] = part[:CR] * scale
        return carry

    lax.fori_loop(0, TR // 2, back_step, 0)

    def igrad_step(n, carry):
        rows = d32[pl.ds(pl.multiple_of(n * 9 * TR, 16), 9 * TR), :]
        ig_v[pl.ds(n * 9, 9)] = rows.reshape(9, TR, TC).astype(BF16)
        return carry

    lax.fori_loop(0, CR // 9, igrad_step, 0)
    store = pltpu.make_async_copy(ig_v, igrad_hbm.at[0], out_sem.at[0])
    store.start()

    home = (reg * 4 + glob) * 2
    wanted = [(home + step + NGB) % NGB for step in (-1, 0, 1, 2, NGB // 2)]
    for i in range(TR):
        cond = bk32[i, CR : CR + BLK, :].astype(BF16).astype(F32)
        target = targets_ref[0, i]
        for n in range(5):
            mask = (target == wanted[n]).astype(F32)
            cmask[n * BLK : (n + 1) * BLK, i * TC : (i + 1) * TC] = (cond * mask).astype(BF16)
    loads[4].wait()
    glob_out[...] = jnp.dot(
        cmask[...], interp_v[...].reshape(TR * TC, TC), preferred_element_type=F32
    ).reshape(5, BLK, TC)
    glob_copies = []
    for n, (block, step) in enumerate(((0, -1), (3, 1), (4, 64))):
        copy = pltpu.make_async_remote_copy(
            glob_out.at[block], glob_recv.at[n], gl_ss.at[n], gl_rs.at[n],
            device_id=flat_dev(step), device_id_type=MESH,
        )
        copy.start()
        glob_copies.append(copy)

    lax.fori_loop(1, 16, lambda d, c: (xy_copy(d).wait_recv(), c)[1], 0)
    piece = acc[pl.ds(pl.multiple_of(q * PIECE, 8), PIECE), :]
    for d in range(1, 16):
        piece = piece + xrecv[d]
    zbuf[z] = piece

    def z_copy(d):
        return pltpu.make_async_remote_copy(
            zbuf.at[z], zbuf.at[z], z_ss.at[d], z_rs.at[d],
            device_id=z_dev(d), device_id_type=MESH,
        )

    def z_arrival(d):
        slot = (z - d + 8) % 8
        return pltpu.make_async_remote_copy(
            zbuf.at[slot], zbuf.at[slot], z_ss.at[d], z_rs.at[d],
            device_id=z_dev(d), device_id_type=MESH,
        )

    lax.fori_loop(1, 8, lambda d, c: (z_copy(d).start(), c)[1], 0)

    for copy in glob_copies:
        copy.wait_recv()
    own[0] = glob_out[1] + glob_recv[1] + glob_recv[2]
    own[1] = glob_out[2] + glob_recv[0]
    cpl_copy = pltpu.make_async_remote_copy(
        own, cplrecv, gl_ss.at[3], gl_rs.at[3], device_id=other, device_id_type=MESH
    )
    cpl_copy.start()

    lax.fori_loop(1, 8, lambda d, c: (z_arrival(d).wait_recv(), c)[1], 0)
    full = zbuf[0]
    for n in range(1, 8):
        full = full + zbuf[n]
    fbuf[:PIECE, :] = full * SCALE_NORM
    fbuf[PIECE:, :] = jnp.zeros((PIECE_B - PIECE, CH), F32)
    gbuf[core, q] = fbuf[...].astype(BF16)

    def ag_copy(d, slot):
        return pltpu.make_async_remote_copy(
            gbuf.at[core, slot], gbuf.at[core, slot], ag_ss.at[d], ag_rs.at[d],
            device_id=plane_dev(d), device_id_type=MESH,
        )

    def source(d):
        return ((x + 4 - d // 4) % 4) * 4 + (y + 4 - d % 4) % 4

    def fw_copy(d, half):
        slot = source(d)
        return pltpu.make_async_remote_copy(
            gbuf.at[half, slot], gbuf.at[half, slot], fw_ss.at[d], fw_rs.at[d],
            device_id=sibling, device_id_type=MESH,
        )

    lax.fori_loop(0, 15, lambda n, c: (ag_copy(15 - n, q).start(), c)[1], 0)
    fw_copy(0, core).start()

    cpl_copy.wait_recv()
    ggrad_ref[...] = (own[...] + cplrecv[...])[:, :CG, :]

    def arrive(d, carry):
        ag_copy(d, source(d)).wait_recv()
        fw_copy(d, core).start()
        return carry

    lax.fori_loop(1, 16, arrive, 0)
    lax.fori_loop(0, 16, lambda d, c: (fw_copy(d, 1 - core).wait_recv(), c)[1], 0)

    for h in range(2):
        for p in range(16):
            part = gbuf[h, p].astype(F32)
            for s in range(PIECE // 8):
                row = p * PIECE + s * 8
                if row >= ROWS_HALF:
                    continue
                k, c = row // HALF, row % HALF + h * HALF
                keep = min(8, CIN - c)
                wgrad_ref[k, c : c + keep, :] = part[s * 8 : s * 8 + keep]
                if h == 1 and k == 0 and c <= CIN < c + 8:
                    bgrad_ref[...] = part[s * 8 + CIN - c : s * 8 + CIN - c + 1]

    store.wait()
    for copy in halo + core_copies + glob_copies + [cpl_copy]:
        copy.wait_send()
    lax.fori_loop(1, 16, lambda d, c: (xy_copy(d).wait_send(), c)[1], 0)
    lax.fori_loop(1, 8, lambda d, c: (z_copy(d).wait_send(), c)[1], 0)
    lax.fori_loop(1, 16, lambda d, c: (ag_copy(d, q).wait_send(), c)[1], 0)
    lax.fori_loop(0, 16, lambda d, c: (fw_copy(d, core).wait_send(), c)[1], 0)


def body(saved_input, pre_act, cotangent, conv_weight, interp, targets, noise_index):
    vmem = pl.BlockSpec(memory_space=pltpu.VMEM)
    smem = pl.BlockSpec(memory_space=pltpu.SMEM)
    any_ = pl.BlockSpec(memory_space=pl.ANY)
    dma = pltpu.SemaphoreType.DMA
    igrad, wgrad, bgrad, ggrad = pl.pallas_call(
        kernel,
        out_shape=(
            jax.ShapeDtypeStruct((1, CR, TR, TC), BF16),
            jax.ShapeDtypeStruct((9, CIN, CH), F32),
            jax.ShapeDtypeStruct((1, CH), F32),
            jax.ShapeDtypeStruct((2, CG, TC), F32),
        ),
        in_specs=[any_] * 5 + [smem] * 2,
        out_specs=(any_, vmem, vmem, vmem),
        scratch_shapes=[
            pltpu.VMEM((CIN, TR, TC), BF16),
            pltpu.VMEM((CH, TR, TC), BF16),
            pltpu.VMEM((CH, TR, TC), BF16),
            pltpu.VMEM((9, CIN, CH), BF16),
            pltpu.VMEM((TR, TC, TC), BF16),
            pltpu.VMEM((CH * TR, TC), F32),
            pltpu.VMEM((CPAD * TR, TC), F32),
            pltpu.VMEM((TR + 2, PITCH, CH), F32),
            pltpu.VMEM(((TR + 2) * TC, 3 * CH), BF16),
            pltpu.VMEM((CPAD, TR * TC), BF16),
            pltpu.VMEM((3, CPAD, 3 * CH), BF16),
            pltpu.VMEM((2, TR, CH), F32),
            pltpu.VMEM((2, TR, CH), F32),
            pltpu.VMEM((2, 2, 8, CH), F32),
            pltpu.VMEM((2, ROWS_HALF, CH), F32),
            pltpu.VMEM((ROWS_HALF, CH), F32),
            pltpu.VMEM((ROWS_ALL, CH), F32),
            pltpu.VMEM((16, PIECE, CH), F32),
            pltpu.VMEM((8, PIECE, CH), F32),
            pltpu.VMEM((PIECE_B, CH), F32),
            pltpu.VMEM((2, 16, PIECE_B, CH), BF16),
            pltpu.VMEM((TR, CPAD + 8, TC), F32),
            pltpu.VMEM((5 * BLK, TR * TC), BF16),
            pltpu.VMEM((5, BLK, TC), F32),
            pltpu.VMEM((3, BLK, TC), F32),
            pltpu.VMEM((2, BLK, TC), F32),
            pltpu.VMEM((2, BLK, TC), F32),
            pltpu.VMEM((CR, TR, TC), BF16),
            dma((5,)),
            dma((8,)),
            dma((8,)),
            dma((3,)),
            dma((3,)),
            dma((16,)),
            dma((16,)),
            dma((8,)),
            dma((8,)),
            dma((16,)),
            dma((16,)),
            dma((16,)),
            dma((16,)),
            dma((4,)),
            dma((4,)),
            dma((1,)),
        ],
        compiler_params=pltpu.CompilerParams(
            collective_id=0, has_side_effects=True, vmem_limit_bytes=40 << 20
        ),
        cost_estimate=pl.CostEstimate(
            flops=2 * 2 * CIN * 9 * CH * TR * TC, bytes_accessed=4 << 20, transcendentals=CH * TR * TC
        ),
    )(saved_input, pre_act, cotangent, conv_weight, interp, targets, noise_index)
    return igrad, wgrad, bgrad.reshape(CH), ggrad


def solution(mesh):
    in_specs = (
        P("cpl", None, "reg", "glob"),
        P("cpl", None, "reg", "glob"),
        P("cpl", None, "reg", "glob"),
        P(),
        P("glob", "reg", None, None),
        P("glob", "reg"),
        P("cpl"),
    )
    out_specs = (P("cpl", None, "reg", "glob"), P(), P(), P(("reg", "glob"), None, None))
    return jax.shard_map(body, mesh=mesh, in_specs=in_specs, out_specs=out_specs, check_vma=False)
```

```python
import math

import jax
import jax.numpy as jnp
from jax import lax
from jax.experimental import pallas as pl
from jax.experimental.pallas import tpu as pltpu
from jax.sharding import PartitionSpec as P

CH = 128
CR = 99
CG = 73
CIN = 172
CPAD = 176
HALF = 88
TR = 16
TC = 128
NGB = 256
NOISE_LEVELS = 18
PIECE = 64
ROWS_HALF = 9 * HALF
ROWS_PAD = 800
ROWS_ALL = 16 * PIECE
TOP = 8
PITCH = TOP + TC + 8
BLK = 80
SCALE_NORM = 1.0 / math.sqrt(512 * 512 * 2)
MESH = pl.DeviceIdType.MESH
F32 = jnp.float32
BF16 = jnp.bfloat16


def kernel(
    saved_hbm, pre_hbm, cot_hbm, w_hbm, interp_hbm, targets_hbm, noise_ref,
    ig_v, gbuf, ggrad_ref,
    saved_v, pre_v, cot_v, w_v, interp_v, targets_ref,
    d32, s32, p32, dzc, smat, wcat, colbuf, colrecv, corner,
    pick, edge, lpad, extra,
    awh, crecv, acc, xrecv, zbuf,
    bk32, cmask, glob_out, glob_recv, own, cplrecv,
    in_sem, halo_ss, halo_rs, core_ss, core_rs, xy_ss, xy_rs, z_ss, z_rs,
    ag_ss, ag_rs, fw_ss, fw_rs, gl_ss, gl_rs,
):
    reg = lax.axis_index("reg")
    glob = lax.axis_index("glob")
    cpl = lax.axis_index("cpl")
    z = reg // 4
    x_lo = (reg // 2) % 2
    core = reg % 2
    x = cpl * 2 + x_lo
    y = glob
    q = x * 4 + y

    def at(x_, y_, z_, core_):
        return {"reg": z_ * 4 + (x_ % 2) * 2 + core_, "glob": y_, "cpl": x_ // 2}

    def plane(d):
        return (x + d // 4) % 4, (y + d % 4) % 4

    def plane_dev(d):
        px, py = plane(d)
        return at(px, py, z, core)

    def z_dev(d):
        return at(x, y, (z + d) % 8, core)

    def halo_dev(dr, dg):
        return {"reg": (reg + dr + 32) % 32, "glob": (glob + dg + 4) % 4, "cpl": cpl}

    def flat_dev(step):
        flat = (reg * 4 + glob + step + 128) % 128
        return {"reg": flat // 4, "glob": flat % 4, "cpl": cpl}

    sibling = at(x, y, z, 1 - core)
    other = {"reg": reg, "glob": glob, "cpl": 1 - cpl}

    loads = [
        pltpu.make_async_copy(src, dst, in_sem.at[n])
        for n, (src, dst) in enumerate((
            (pre_hbm.at[0], pre_v),
            (cot_hbm.at[0], cot_v),
            (saved_hbm.at[0], saved_v),
            (w_hbm, w_v),
            (interp_hbm.at[0], interp_v),
            (targets_hbm, targets_ref),
        ))
    ]
    for load in loads:
        load.start()
    pend = {n: load.wait for n, load in enumerate(loads)}

    barrier = pltpu.get_barrier_semaphore()

    def greet(device):
        pl.semaphore_signal(barrier, inc=1, device_id=device, device_id_type=MESH)

    halo_steps = [(dr, dg) for dr in (-1, 0, 1) for dg in (-1, 0, 1) if dr or dg]
    for dr, dg in halo_steps:
        greet(halo_dev(dr, dg))
    for step in (-1, 1, 64):
        greet(flat_dev(step))
    greet(other)
    greet(sibling)
    lax.fori_loop(1, 16, lambda d, c: (greet(plane_dev(d)), c)[1], 0)
    lax.fori_loop(1, 8, lambda d, c: (greet(z_dev(d)), c)[1], 0)

    s32[CIN * TR :, :] = jnp.zeros((CPAD * TR - CIN * TR, TC), F32)
    wcat[:, CPAD - 16 :, :] = jnp.zeros((3, 16, 3 * CH), BF16)
    acc[ROWS_PAD:, :] = jnp.zeros((ROWS_ALL - ROWS_PAD, CH), BF16)
    awh[:, ROWS_HALF:, :] = jnp.zeros((2, ROWS_PAD - ROWS_HALF, CH), F32)
    crecv[ROWS_HALF:, :] = jnp.zeros((ROWS_PAD - ROWS_HALF, CH), F32)
    for i in range(TR):
        p32[i + 1, :TOP, :] = jnp.zeros((TOP, CH), F32)
        p32[i + 1, TOP + TC :, :] = jnp.zeros((8, CH), F32)
    lpad[...] = jnp.zeros((2, 24, CH), F32)
    extra[...] = jnp.zeros((3, TC, 3 * CH), BF16)
    bk32[:, CPAD:, :] = jnp.zeros((TR, 8, TC), F32)

    pend.pop(0)()
    pend.pop(1)()

    def silu_step(n, carry):
        pre = pre_v[pl.ds(n * 8, 8)].astype(F32)
        cot = cot_v[pl.ds(n * 8, 8)].astype(F32)
        sig = 0.5 * jnp.tanh(0.5 * pre) + 0.5
        dz = cot * sig * (1.0 + pre * (1.0 - sig))
        d32[pl.ds(pl.multiple_of(n * 8 * TR, 128), 8 * TR), :] = dz.reshape(8 * TR, TC)
        return carry

    lax.fori_loop(0, CH // 8, silu_step, 0)

    def turn(i):
        tile = jnp.transpose(d32[pl.ds(i, CH, stride=TR), :], (1, 0))
        p32[i + 1, TOP : TOP + TC, :] = tile
        colbuf[0, i : i + 1, :] = tile[:1]
        colbuf[1, i : i + 1, :] = tile[TC - 1 :]
        return tile

    total = jnp.zeros((TC, CH), F32)
    for i in range(TR):
        total = total + turn(i)
    bias = jnp.sum(total, axis=0, keepdims=True)

    pl.semaphore_wait(barrier, 8 + 3 + 1 + 1 + 15 + 7)

    for dr, dg in halo_steps:
        row = TR if dr > 0 else 1
        if dg == 0:
            kind = 0
            src = p32.at[row, pl.ds(TOP, TC)]
            dst = p32.at[0 if dr > 0 else TR + 1, pl.ds(TOP, TC)]
        elif dr == 0:
            kind = 1
            src = colbuf.at[1 if dg > 0 else 0]
            dst = colrecv.at[0 if dg > 0 else 1]
        else:
            kind = 2
            src = p32.at[row, pl.ds(TOP + TC - 8 if dg > 0 else TOP, 8)]
            dst = corner.at[0 if dr > 0 else 1, 0 if dg > 0 else 1]
        pltpu.make_async_remote_copy(
            src, dst, halo_ss.at[kind], halo_rs.at[kind],
            device_id=halo_dev(dr, dg), device_id_type=MESH,
        ).start()

    def bulk(ref, sem):
        return pltpu.make_async_copy(ref, ref, sem).wait

    halo_bulk = (d32.at[pl.ds(0, 2 * TC)], colrecv, corner)
    for kind in range(3):
        pend["halo_s", kind] = bulk(halo_bulk[kind], halo_ss.at[kind])
        pend["halo", kind] = bulk(halo_bulk[kind], halo_rs.at[kind])

    pend.pop(2)()

    def saved_step(n, carry):
        part = saved_v[pl.ds(n * 4, 4)].astype(F32)
        s32[pl.ds(pl.multiple_of(n * 4 * TR, 64), 4 * TR), :] = part.reshape(4 * TR, TC)
        return carry

    lax.fori_loop(0, CIN // 4, saved_step, 0)
    for i in range(TR):
        smat[:, i * TC : (i + 1) * TC] = s32[pl.ds(i, CPAD, stride=TR), :].astype(BF16)

    def shift_rows(i):
        for bi in range(3):
            dzc[pl.ds(pl.multiple_of(i * TC, TC), TC), bi * CH : (bi + 1) * CH] = p32[
                i, TOP + 1 - bi : TOP + 1 - bi + TC, :
            ].astype(BF16)

    lax.fori_loop(1, TR + 1, lambda i, c: (shift_rows(i), c)[1], 0)
    border = jnp.zeros((TC, 3 * CH), BF16)
    dzc[:TC, :] = border
    dzc[(TR + 1) * TC :, :] = border
    for a in range(3):
        term = jnp.dot(
            smat[...], dzc[(2 - a) * TC : (2 - a) * TC + TR * TC, :],
            preferred_element_type=F32,
        )
        for bi in range(3):
            k = 3 * a + bi
            for h in range(2):
                awh[h, k * HALF : (k + 1) * HALF, :] = term[
                    h * HALF : (h + 1) * HALF, bi * CH : (bi + 1) * CH
                ]
    awh[1, CIN - HALF : CIN - HALF + 1, :] = bias

    at_row = lax.broadcasted_iota(jnp.int32, (TC, TC), 0)
    at_lane = lax.broadcasted_iota(jnp.int32, (TC, TC), 1)
    for i in range(TR):
        first = (at_row == 0) & (at_lane == i)
        last = (at_row == TC - 1) & (at_lane == TR + i)
        pick[i * TC : (i + 1) * TC, :] = jnp.where(first | last, 1.0, 0.0).astype(BF16)
    edge[...] = jnp.dot(smat[...], pick[...], preferred_element_type=F32).astype(BF16)

    pend.pop(3)()
    for a in range(3):
        for bi in range(3):
            wcat[a, :CIN, bi * CH : (bi + 1) * CH] = w_v[3 * a + bi]

    for kind in range(3):
        pend.pop(("halo", kind))()
    up = (reg > 0).astype(F32)
    down = (reg < 31).astype(F32)
    left = (glob > 0).astype(F32)
    right = (glob < 3).astype(F32)
    p32[0, TOP : TOP + TC, :] = p32[0, TOP : TOP + TC, :] * up
    p32[TR + 1, TOP : TOP + TC, :] = p32[TR + 1, TOP : TOP + TC, :] * down
    lpad[0, 1 : TR + 1, :] = colrecv[0] * left
    lpad[1, 1 : TR + 1, :] = colrecv[1] * right
    for i in range(TR):
        p32[i + 1, TOP - 1 : TOP, :] = lpad[0, i + 1 : i + 2, :]
        p32[i + 1, TOP + TC : TOP + TC + 1, :] = lpad[1, i + 1 : i + 2, :]
    p32[0, TOP - 1 : TOP, :] = corner[0, 0, 7:8, :] * (up * left)
    p32[0, TOP + TC : TOP + TC + 1, :] = corner[0, 1, 0:1, :] * (up * right)
    p32[TR + 1, TOP - 1 : TOP, :] = corner[1, 0, 7:8, :] * (down * left)
    p32[TR + 1, TOP + TC : TOP + TC + 1, :] = corner[1, 1, 0:1, :] * (down * right)
    shift_rows(0)
    shift_rows(TR + 1)
    for a in range(3):
        extra[a, :TR, 2 * CH :] = lpad[0, 2 - a : 2 - a + TR, :].astype(BF16)
        extra[a, TR : 2 * TR, :CH] = lpad[1, 2 - a : 2 - a + TR, :].astype(BF16)

    for a in range(3):
        term = jnp.dot(edge[...], extra[a], preferred_element_type=F32)
        if a == 0:
            term = term + jnp.dot(
                smat[:, (TR - 1) * TC :], dzc[(TR + 1) * TC :, :], preferred_element_type=F32
            )
        if a == 2:
            term = term + jnp.dot(smat[:, :TC], dzc[:TC, :], preferred_element_type=F32)
        for bi in range(3):
            k = 3 * a + bi
            for h in range(2):
                rows = slice(k * HALF, (k + 1) * HALF)
                awh[h, rows, :] = awh[h, rows, :] + term[
                    h * HALF : (h + 1) * HALF, bi * CH : (bi + 1) * CH
                ]
        if a == 0:
            awh[1, CIN - HALF : CIN - HALF + 1, :] = bias
        rows = pl.ds(3 * a * HALF, 3 * HALF)
        pltpu.make_async_remote_copy(
            awh.at[1 - core, rows], crecv.at[rows], core_ss, core_rs,
            device_id=sibling, device_id_type=MESH,
        ).start()
    pend["core_s"] = bulk(crecv.at[pl.ds(0, ROWS_HALF)], core_ss)
    pend["core"] = bulk(crecv.at[pl.ds(0, ROWS_HALF)], core_rs)
    lax.fori_loop(1, TR + 1, lambda i, c: (shift_rows(i), c)[1], 0)
    pend.pop("core")()
    acc[:ROWS_PAD, :] = (awh[core] + crecv[...]).astype(BF16)
    def xy_start(n, carry):
        d = 15 - n
        px, py = plane(d)
        pltpu.make_async_remote_copy(
            acc.at[pl.ds(pl.multiple_of((px * 4 + py) * PIECE, PIECE), PIECE)],
            xrecv.at[d], xy_ss, xy_rs,
            device_id=at(px, py, z, core), device_id_type=MESH,
        ).start()
        return carry

    lax.fori_loop(0, 15, xy_start, 0)
    pend["xy_s"] = bulk(xrecv.at[pl.ds(1, 15)], xy_ss)
    pend["xy"] = bulk(xrecv.at[pl.ds(1, 15)], xy_rs)

    level = jnp.full((1, TC), noise_ref[0], jnp.int32).astype(F32) / (NOISE_LEVELS - 1)
    sigma = jnp.exp(math.log(2.0) + level * (math.log(0.05) - math.log(2.0)))
    scale = 1.0 / jnp.sqrt(sigma * sigma + 0.25)

    def back_step(n, carry):
        back = jnp.zeros((CPAD, 2 * TC), F32)
        for a in range(3):
            start = pl.multiple_of((2 * n + 2 - a) * TC, TC)
            back = back + lax.dot_general(
                wcat[a], dzc[pl.ds(start, 2 * TC), :], (((1,), (1,)), ((), ())),
                preferred_element_type=F32,
            )
        for half in range(2):
            part = back[:, half * TC : (half + 1) * TC]
            bk32[2 * n + half, :CPAD, :] = part
            d32[pl.ds(2 * n + half, CR, stride=TR), :] = part[:CR] * scale
        return carry

    lax.fori_loop(0, TR // 2, back_step, 0)

    def igrad_step(n, carry):
        rows = d32[pl.ds(pl.multiple_of(n * 9 * TR, 16), 9 * TR), :]
        ig_v[pl.ds(n * 9, 9)] = rows.reshape(9, TR, TC).astype(BF16)
        return carry

    lax.fori_loop(0, CR // 9, igrad_step, 0)
    pend.pop(5)()
    home = (reg * 4 + glob) * 2
    wanted = [(home + step + NGB) % NGB for step in (-1, 0, 1, 2, NGB // 2)]
    for i in range(TR):
        cond = bk32[i, CR : CR + BLK, :].astype(BF16).astype(F32)
        target = targets_ref[0, i]
        for n in range(5):
            mask = (target == wanted[n]).astype(F32)
            cmask[n * BLK : (n + 1) * BLK, i * TC : (i + 1) * TC] = (cond * mask).astype(BF16)
    pend.pop(4)()
    glob_out[...] = jnp.dot(
        cmask[...], interp_v[...].reshape(TR * TC, TC), preferred_element_type=F32
    ).reshape(5, BLK, TC)
    for n, (block, step) in enumerate(((0, -1), (3, 1), (4, 64))):
        pltpu.make_async_remote_copy(
            glob_out.at[block], glob_recv.at[n], gl_ss.at[0], gl_rs.at[0],
            device_id=flat_dev(step), device_id_type=MESH,
        ).start()
    pend["glob_s"] = bulk(glob_recv, gl_ss.at[0])
    pend["glob"] = bulk(glob_recv, gl_rs.at[0])
    pend.pop("xy")()
    piece = acc[pl.ds(pl.multiple_of(q * PIECE, PIECE), PIECE), :].astype(F32)
    for d in range(1, 16):
        piece = piece + xrecv[d].astype(F32)
    zbuf[z] = piece.astype(BF16)

    def z_start(d, carry):
        pltpu.make_async_remote_copy(
            zbuf.at[z], zbuf.at[z], z_ss, z_rs, device_id=z_dev(d), device_id_type=MESH
        ).start()
        return carry

    lax.fori_loop(1, 8, z_start, 0)
    pend["z_s"] = bulk(zbuf.at[pl.ds(0, 7)], z_ss)
    pend["z"] = bulk(zbuf.at[pl.ds(0, 7)], z_rs)

    pend.pop("glob")()
    own[0] = glob_out[1] + glob_recv[1] + glob_recv[2]
    own[1] = glob_out[2] + glob_recv[0]
    cpl_copy = pltpu.make_async_remote_copy(
        own, cplrecv, gl_ss.at[1], gl_rs.at[1], device_id=other, device_id_type=MESH
    )
    cpl_copy.start()
    pend["cpl_s"] = cpl_copy.wait_send
    pend["cpl"] = cpl_copy.wait_recv

    pend.pop("z")()
    full = zbuf[0].astype(F32)
    for n in range(1, 8):
        full = full + zbuf[n].astype(F32)
    gbuf[core, q] = (full * SCALE_NORM).astype(BF16)

    def ag_start(n, carry):
        d = 15 - n
        pltpu.make_async_remote_copy(
            gbuf.at[core, q], gbuf.at[core, q], ag_ss, ag_rs.at[d // 4],
            device_id=plane_dev(d), device_id_type=MESH,
        ).start()
        return carry

    lax.fori_loop(0, 15, ag_start, 0)
    pend["ag_s"] = bulk(gbuf.at[0, pl.ds(0, 15)], ag_ss)

    pend.pop("cpl")()
    ggrad_ref[...] = own[...] + cplrecv[...]

    for dx in (0, 1, 3, 2):
        count = 3 if dx == 0 else 4
        bulk(gbuf.at[0, pl.ds(0, count)], ag_rs.at[dx])()
        column = gbuf.at[core, pl.ds(lax.rem(x + 4 - dx, 4) * 4, 4)]
        pltpu.make_async_remote_copy(
            column, column, fw_ss, fw_rs, device_id=sibling, device_id_type=MESH
        ).start()
    pend["fw_s"] = bulk(gbuf.at[0], fw_ss)
    bulk(gbuf.at[0], fw_rs)()
    for wait in pend.values():
        wait()


def finish(ig_v, gbuf, gg_v, igrad_hbm, wgrad_hbm, bgrad_hbm, ggrad_hbm, w32, b32, g32, sem):
    first = pltpu.make_async_copy(ig_v, igrad_hbm.at[0], sem.at[0])
    first.start()
    for n in range(2):
        g32[:, n : n + 1, :] = gg_v[n, :CG, :].reshape(CG, 1, TC)
    second = pltpu.make_async_copy(g32, ggrad_hbm, sem.at[1])
    second.start()
    for h in range(2):
        for p in range(16):
            part = gbuf[h, p].astype(F32)
            for s in range(PIECE // 8):
                row = p * PIECE + s * 8
                if row >= ROWS_HALF:
                    continue
                k, c = row // HALF, row % HALF + h * HALF
                keep = min(8, CIN - c)
                w32[k, c : c + keep, :] = part[s * 8 : s * 8 + keep]
                if h == 1 and k == 0 and c <= CIN < c + 8:
                    b32[...] = part[s * 8 + CIN - c]

    third = pltpu.make_async_copy(w32, wgrad_hbm, sem.at[2])
    third.start()
    fourth = pltpu.make_async_copy(b32, bgrad_hbm, sem.at[3])
    fourth.start()
    for copy in (first, second, third, fourth):
        copy.wait()


def body(saved_input, pre_act, cotangent, conv_weight, interp, targets, noise_index):
    vmem = pl.BlockSpec(memory_space=pltpu.VMEM)
    smem = pl.BlockSpec(memory_space=pltpu.SMEM)
    hbm = pl.BlockSpec(memory_space=pltpu.HBM)
    dma = pltpu.SemaphoreType.DMA
    pinned = [
        pltpu.with_memory_space_constraint(v, pltpu.HBM)
        for v in (saved_input, pre_act, cotangent, conv_weight, interp, targets)
    ]
    parts = pl.pallas_call(
        kernel,
        out_shape=(
            jax.ShapeDtypeStruct((CR, TR, TC), BF16),
            jax.ShapeDtypeStruct((2, 16, PIECE, CH), BF16),
            jax.ShapeDtypeStruct((2, BLK, TC), F32),
        ),
        in_specs=[hbm] * 6 + [smem],
        out_specs=(vmem, vmem, vmem),
        scratch_shapes=[
            pltpu.VMEM((CIN, TR, TC), BF16),
            pltpu.VMEM((CH, TR, TC), BF16),
            pltpu.VMEM((CH, TR, TC), BF16),
            pltpu.VMEM((9, CIN, CH), BF16),
            pltpu.VMEM((TR, TC, TC), BF16),
            pltpu.SMEM((1, TR), jnp.int32),
            pltpu.VMEM((CH * TR, TC), F32),
            pltpu.VMEM((CPAD * TR, TC), F32),
            pltpu.VMEM((TR + 2, PITCH, CH), F32),
            pltpu.VMEM(((TR + 2) * TC, 3 * CH), BF16),
            pltpu.VMEM((CPAD, TR * TC), BF16),
            pltpu.VMEM((3, CPAD, 3 * CH), BF16),
            pltpu.VMEM((2, TR, CH), F32),
            pltpu.VMEM((2, TR, CH), F32),
            pltpu.VMEM((2, 2, 8, CH), F32),
            pltpu.VMEM((TR * TC, TC), BF16),
            pltpu.VMEM((CPAD, TC), BF16),
            pltpu.VMEM((2, 24, CH), F32),
            pltpu.VMEM((3, TC, 3 * CH), BF16),
            pltpu.VMEM((2, ROWS_PAD, CH), F32),
            pltpu.VMEM((ROWS_PAD, CH), F32),
            pltpu.VMEM((ROWS_ALL, CH), BF16),
            pltpu.VMEM((16, PIECE, CH), BF16),
            pltpu.VMEM((8, PIECE, CH), BF16),
            pltpu.VMEM((TR, CPAD + 8, TC), F32),
            pltpu.VMEM((5 * BLK, TR * TC), BF16),
            pltpu.VMEM((5, BLK, TC), F32),
            pltpu.VMEM((3, BLK, TC), F32),
            pltpu.VMEM((2, BLK, TC), F32),
            pltpu.VMEM((2, BLK, TC), F32),
            dma((6,)),
            dma((3,)),
            dma((3,)),
            dma,
            dma,
            dma,
            dma,
            dma,
            dma,
            dma,
            dma((4,)),
            dma,
            dma,
            dma((2,)),
            dma((2,)),
        ],
        compiler_params=pltpu.CompilerParams(
            collective_id=0, has_side_effects=True, vmem_limit_bytes=40 << 20
        ),
        cost_estimate=pl.CostEstimate(
            flops=2 * 2 * CIN * 9 * CH * TR * TC, bytes_accessed=4 << 20, transcendentals=CH * TR * TC
        ),
    )(*pinned, noise_index)
    igrad, wgrad, bgrad, ggrad = pl.pallas_call(
        finish,
        out_shape=(
            pltpu.HBM((1, CR, TR, TC), BF16),
            pltpu.HBM((9, CIN, CH), F32),
            pltpu.HBM((CH,), F32),
            pltpu.HBM((CG, 2, TC), F32),
        ),
        in_specs=[vmem] * 3,
        out_specs=(hbm, hbm, hbm, hbm),
        scratch_shapes=[
            pltpu.VMEM((9, CIN, CH), F32),
            pltpu.VMEM((CH,), F32),
            pltpu.VMEM((CG, 2, TC), F32),
            dma((4,)),
        ],
        compiler_params=pltpu.CompilerParams(vmem_limit_bytes=16 << 20),
    )(*parts)
    return igrad, wgrad, bgrad, jnp.transpose(ggrad, (1, 0, 2))


def solution(mesh):
    in_specs = (
        P("cpl", None, "reg", "glob"),
        P("cpl", None, "reg", "glob"),
        P("cpl", None, "reg", "glob"),
        P(),
        P("glob", "reg", None, None),
        P("glob", "reg"),
        P("cpl"),
    )
    out_specs = (P("cpl", None, "reg", "glob"), P(), P(), P(("reg", "glob"), None, None))
    return jax.shard_map(body, mesh=mesh, in_specs=in_specs, out_specs=out_specs, check_vma=False)
```

```python
import math

import jax
import jax.numpy as jnp
from jax import lax
from jax.experimental import pallas as pl
from jax.experimental.pallas import tpu as pltpu
from jax.sharding import PartitionSpec as P

CH = 128
CR = 99
CG = 73
CIN = 172
CPAD = 176
HALF = 88
TR = 16
TC = 128
NGB = 256
NOISE_LEVELS = 18
PIECE = 64
ROWS_HALF = 9 * HALF
ROWS_PAD = 800
ROWS_ALL = 16 * PIECE
TOP = 8
PITCH = TOP + TC + 8
BLK = 80
SCALE_NORM = 1.0 / math.sqrt(512 * 512 * 2)
PLANE = (10, 9, 11, 6, 14, 8, 2, 5, 7, 13, 15, 4, 12, 1, 3)
MESH = pl.DeviceIdType.MESH
F32 = jnp.float32
BF16 = jnp.bfloat16


def kernel(
    saved_hbm, pre_hbm, cot_hbm, w_hbm, interp_hbm, targets_hbm, noise_ref,
    ig_v, gbuf, ggrad_ref,
    saved_v, pre_v, cot_v, w_v, interp_v, targets_ref,
    d32, s32, p32, dzc, smat, wcat, colbuf, colrecv, corner,
    rows_out, rows_in, pick, edge, lpad, extra,
    awh, crecv, acc, xrecv, zbuf,
    bk32, cmask, glob_out, glob_recv, own, cplrecv,
    in_sem, halo_ss, halo_rs, core_ss, core_rs, xy_ss, xy_rs, z_ss, z_rs,
    ag_ss, ag_rs, fw_ss, fw_rs, gl_ss, gl_rs,
):
    reg = lax.axis_index("reg")
    glob = lax.axis_index("glob")
    cpl = lax.axis_index("cpl")
    z = reg // 4
    x_lo = (reg // 2) % 2
    core = reg % 2
    x = cpl * 2 + x_lo
    y = glob
    q = x * 4 + y

    def at(x_, y_, z_, core_):
        return {"reg": z_ * 4 + (x_ % 2) * 2 + core_, "glob": y_, "cpl": x_ // 2}

    def plane(d):
        return (x + d // 4) % 4, (y + d % 4) % 4

    def plane_dev(d):
        px, py = plane(d)
        return at(px, py, z, core)

    def z_dev(d):
        return at(x, y, (z + d) % 8, core)

    def halo_dev(dr, dg):
        return {"reg": (reg + dr + 32) % 32, "glob": (glob + dg + 4) % 4, "cpl": cpl}

    def flat_dev(step):
        flat = (reg * 4 + glob + step + 128) % 128
        return {"reg": flat // 4, "glob": flat % 4, "cpl": cpl}

    sibling = at(x, y, z, 1 - core)
    other = {"reg": reg, "glob": glob, "cpl": 1 - cpl}

    loads = [
        pltpu.make_async_copy(src, dst, in_sem.at[n])
        for n, (src, dst) in enumerate((
            (pre_hbm.at[0], pre_v),
            (cot_hbm.at[0], cot_v),
            (saved_hbm.at[0], saved_v),
            (w_hbm, w_v),
            (interp_hbm.at[0], interp_v),
            (targets_hbm, targets_ref),
        ))
    ]
    for load in loads:
        load.start()
    pend = {n: load.wait for n, load in enumerate(loads)}

    barrier = pltpu.get_barrier_semaphore()

    def greet(device):
        pl.semaphore_signal(barrier, inc=1, device_id=device, device_id_type=MESH)

    halo_steps = [(dr, dg) for dr in (-1, 0, 1) for dg in (-1, 0, 1) if dr or dg]
    for dr, dg in halo_steps:
        greet(halo_dev(dr, dg))
    for step in (-1, 1, 64):
        greet(flat_dev(step))
    greet(other)
    greet(sibling)
    lax.fori_loop(1, 16, lambda d, c: (greet(plane_dev(d)), c)[1], 0)
    lax.fori_loop(1, 8, lambda d, c: (greet(z_dev(d)), c)[1], 0)

    s32[CIN * TR :, :] = jnp.zeros((CPAD * TR - CIN * TR, TC), F32)
    wcat[:, CPAD - 16 :, :] = jnp.zeros((3, 16, 3 * CH), BF16)
    acc[ROWS_PAD:, :] = jnp.zeros((ROWS_ALL - ROWS_PAD, CH), BF16)
    awh[:, ROWS_HALF:, :] = jnp.zeros((2, ROWS_PAD - ROWS_HALF, CH), F32)
    crecv[ROWS_HALF:, :] = jnp.zeros((ROWS_PAD - ROWS_HALF, CH), F32)
    for i in range(TR):
        p32[i + 1, :TOP, :] = jnp.zeros((TOP, CH), F32)
        p32[i + 1, TOP + TC :, :] = jnp.zeros((8, CH), F32)
    lpad[...] = jnp.zeros((2, 24, CH), F32)
    extra[...] = jnp.zeros((3, TC, 3 * CH), BF16)
    bk32[:, CPAD:, :] = jnp.zeros((TR, 8, TC), F32)

    pend.pop(0)()
    pend.pop(1)()

    def silu_step(n, carry):
        pre = pre_v[pl.ds(n * 8, 8)].astype(F32)
        cot = cot_v[pl.ds(n * 8, 8)].astype(F32)
        sig = 0.5 * jnp.tanh(0.5 * pre) + 0.5
        dz = cot * sig * (1.0 + pre * (1.0 - sig))
        d32[pl.ds(pl.multiple_of(n * 8 * TR, 128), 8 * TR), :] = dz.reshape(8 * TR, TC)
        return carry

    lax.fori_loop(0, CH // 8, silu_step, 0)

    def turn(i):
        tile = jnp.transpose(d32[pl.ds(i, CH, stride=TR), :], (1, 0))
        p32[i + 1, TOP : TOP + TC, :] = tile
        colbuf[0, i : i + 1, :] = tile[:1]
        colbuf[1, i : i + 1, :] = tile[TC - 1 :]
        return tile

    total = jnp.zeros((TC, CH), F32)
    for i in range(TR):
        total = total + turn(i)
    bias = jnp.sum(total, axis=0, keepdims=True)

    pend.pop(2)()

    def saved_step(n, carry):
        part = saved_v[pl.ds(n * 4, 4)].astype(F32)
        s32[pl.ds(pl.multiple_of(n * 4 * TR, 64), 4 * TR), :] = part.reshape(4 * TR, TC)
        return carry

    lax.fori_loop(0, CIN // 4, saved_step, 0)
    rows_out[0] = s32[pl.ds(0, CPAD, stride=TR), :].astype(BF16)
    rows_out[1] = s32[pl.ds(TR - 1, CPAD, stride=TR), :].astype(BF16)

    pl.semaphore_wait(barrier, 8 + 3 + 1 + 1 + 15 + 7)

    def send(src, dst, kind, dr, dg):
        pltpu.make_async_remote_copy(
            src, dst, halo_ss.at[kind], halo_rs.at[kind],
            device_id=halo_dev(dr, dg), device_id_type=MESH,
        ).start()

    def bulk(ref, sem):
        return pltpu.make_async_copy(ref, ref, sem).wait

    send(rows_out.at[0], rows_in.at[1], 0, -1, 0)
    send(rows_out.at[1], rows_in.at[0], 0, 1, 0)
    send(colbuf.at[0], colrecv.at[1], 1, 0, -1)
    send(colbuf.at[1], colrecv.at[0], 1, 0, 1)
    halo_bulk = (rows_in, colrecv, d32.at[pl.ds(0, 2 * TC)], corner)
    for kind in range(4):
        pend["halo_s", kind] = bulk(halo_bulk[kind], halo_ss.at[kind])
        pend["halo", kind] = bulk(halo_bulk[kind], halo_rs.at[kind])

    for i in range(TR):
        smat[:, i * TC : (i + 1) * TC] = s32[pl.ds(i, CPAD, stride=TR), :].astype(BF16)

    def shift_rows(i):
        for bi in range(3):
            dzc[pl.ds(pl.multiple_of(i * TC, TC), TC), bi * CH : (bi + 1) * CH] = p32[
                i, TOP + 1 - bi : TOP + 1 - bi + TC, :
            ].astype(BF16)

    lax.fori_loop(1, TR + 1, lambda i, c: (shift_rows(i), c)[1], 0)
    for a in range(3):
        first, count = max(a - 1, 0), TR - abs(a - 1)
        start = TC * (first + 2 - a)
        term = jnp.dot(
            smat[:, first * TC : (first + count) * TC], dzc[start : start + count * TC, :],
            preferred_element_type=F32,
        )
        for bi in range(3):
            k = 3 * a + bi
            for h in range(2):
                awh[h, k * HALF : (k + 1) * HALF, :] = term[
                    h * HALF : (h + 1) * HALF, bi * CH : (bi + 1) * CH
                ]

    for dr, dg in halo_steps:
        row = TR if dr > 0 else 1
        if dg == 0:
            dst = p32.at[0 if dr > 0 else TR + 1, pl.ds(TOP, TC)]
            send(p32.at[row, pl.ds(TOP, TC)], dst, 2, dr, dg)
        elif dr != 0:
            dst = corner.at[0 if dr > 0 else 1, 0 if dg > 0 else 1]
            send(p32.at[row, pl.ds(TOP + TC - 8 if dg > 0 else TOP, 8)], dst, 3, dr, dg)

    at_row = lax.broadcasted_iota(jnp.int32, (TC, TC), 0)
    at_lane = lax.broadcasted_iota(jnp.int32, (TC, TC), 1)
    for i in range(TR):
        first = (at_row == 0) & (at_lane == i)
        last = (at_row == TC - 1) & (at_lane == TR + i)
        pick[i * TC : (i + 1) * TC, :] = jnp.where(first | last, 1.0, 0.0).astype(BF16)
    edge[...] = jnp.dot(smat[...], pick[...], preferred_element_type=F32).astype(BF16)

    pend.pop(("halo", 0))()
    pend.pop(("halo", 1))()
    up = (reg > 0).astype(F32)
    down = (reg < 31).astype(F32)
    left = (glob > 0).astype(F32)
    right = (glob < 3).astype(F32)
    lpad[0, 1 : TR + 1, :] = colrecv[0] * left
    lpad[1, 1 : TR + 1, :] = colrecv[1] * right
    for i in range(TR):
        p32[i + 1, TOP - 1 : TOP, :] = lpad[0, i + 1 : i + 2, :]
        p32[i + 1, TOP + TC : TOP + TC + 1, :] = lpad[1, i + 1 : i + 2, :]
    shift_rows(1)
    shift_rows(TR)
    for a in range(3):
        extra[a, :TR, 2 * CH :] = lpad[0, 2 - a : 2 - a + TR, :].astype(BF16)
        extra[a, TR : 2 * TR, :CH] = lpad[1, 2 - a : 2 - a + TR, :].astype(BF16)

    for a in range(3):
        term = jnp.dot(edge[...], extra[a], preferred_element_type=F32)
        if a == 0:
            term = term + up * jnp.dot(
                rows_in[0], dzc[TC : 2 * TC, :], preferred_element_type=F32
            )
        if a == 2:
            term = term + down * jnp.dot(
                rows_in[1], dzc[TR * TC : (TR + 1) * TC, :], preferred_element_type=F32
            )
        for bi in range(3):
            k = 3 * a + bi
            for h in range(2):
                rows = slice(k * HALF, (k + 1) * HALF)
                awh[h, rows, :] = awh[h, rows, :] + term[
                    h * HALF : (h + 1) * HALF, bi * CH : (bi + 1) * CH
                ]
        if a == 0:
            awh[1, CIN - HALF : CIN - HALF + 1, :] = bias
        rows = pl.ds(3 * a * HALF, 3 * HALF)
        pltpu.make_async_remote_copy(
            awh.at[1 - core, rows], crecv.at[rows], core_ss, core_rs,
            device_id=sibling, device_id_type=MESH,
        ).start()
    pend["core_s"] = bulk(crecv.at[pl.ds(0, ROWS_HALF)], core_ss)
    pend["core"] = bulk(crecv.at[pl.ds(0, ROWS_HALF)], core_rs)
    pend.pop("core")()
    acc[:ROWS_PAD, :] = (awh[core] + crecv[...]).astype(BF16)
    for d in PLANE:
        px, py = plane(d)
        pltpu.make_async_remote_copy(
            acc.at[pl.ds(pl.multiple_of((px * 4 + py) * PIECE, PIECE), PIECE)],
            xrecv.at[d], xy_ss, xy_rs,
            device_id=at(px, py, z, core), device_id_type=MESH,
        ).start()
    pend["xy_s"] = bulk(xrecv.at[pl.ds(1, 15)], xy_ss)
    pend["xy"] = bulk(xrecv.at[pl.ds(1, 15)], xy_rs)
    pend.pop(3)()
    for a in range(3):
        for bi in range(3):
            wcat[a, :CIN, bi * CH : (bi + 1) * CH] = w_v[3 * a + bi]
    lax.fori_loop(2, TR, lambda i, c: (shift_rows(i), c)[1], 0)

    level = jnp.full((1, TC), noise_ref[0], jnp.int32).astype(F32) / (NOISE_LEVELS - 1)
    sigma = jnp.exp(math.log(2.0) + level * (math.log(0.05) - math.log(2.0)))
    scale = 1.0 / jnp.sqrt(sigma * sigma + 0.25)

    def back_step(n, carry):
        back = jnp.zeros((CPAD, 2 * TC), F32)
        for a in range(3):
            start = pl.multiple_of((2 * n + 2 - a) * TC, TC)
            back = back + lax.dot_general(
                wcat[a], dzc[pl.ds(start, 2 * TC), :], (((1,), (1,)), ((), ())),
                preferred_element_type=F32,
            )
        for half in range(2):
            part = back[:, half * TC : (half + 1) * TC]
            bk32[2 * n + half, :CPAD, :] = part
            d32[pl.ds(2 * n + half, CR, stride=TR), :] = part[:CR] * scale
        return carry

    lax.fori_loop(1, TR // 2 - 1, back_step, 0)

    pend.pop("xy")()
    piece = acc[pl.ds(pl.multiple_of(q * PIECE, PIECE), PIECE), :].astype(F32)
    for d in range(1, 16):
        piece = piece + xrecv[d].astype(F32)
    zbuf[z] = piece.astype(BF16)

    for d in (4, 3, 5, 2, 6, 1, 7):
        pltpu.make_async_remote_copy(
            zbuf.at[z], zbuf.at[z], z_ss, z_rs, device_id=z_dev(d), device_id_type=MESH
        ).start()
    pend["z_s"] = bulk(zbuf.at[pl.ds(0, 7)], z_ss)
    pend["z"] = bulk(zbuf.at[pl.ds(0, 7)], z_rs)

    pend.pop(("halo", 2))()
    pend.pop(("halo", 3))()
    p32[0, TOP : TOP + TC, :] = p32[0, TOP : TOP + TC, :] * up
    p32[TR + 1, TOP : TOP + TC, :] = p32[TR + 1, TOP : TOP + TC, :] * down
    p32[0, TOP - 1 : TOP, :] = corner[0, 0, 7:8, :] * (up * left)
    p32[0, TOP + TC : TOP + TC + 1, :] = corner[0, 1, 0:1, :] * (up * right)
    p32[TR + 1, TOP - 1 : TOP, :] = corner[1, 0, 7:8, :] * (down * left)
    p32[TR + 1, TOP + TC : TOP + TC + 1, :] = corner[1, 1, 0:1, :] * (down * right)
    shift_rows(0)
    shift_rows(TR + 1)

    back_step(0, 0)
    back_step(TR // 2 - 1, 0)

    def igrad_step(n, carry):
        rows = d32[pl.ds(pl.multiple_of(n * 9 * TR, 16), 9 * TR), :]
        ig_v[pl.ds(n * 9, 9)] = rows.reshape(9, TR, TC).astype(BF16)
        return carry

    lax.fori_loop(0, CR // 9, igrad_step, 0)
    pend.pop(5)()
    home = (reg * 4 + glob) * 2
    wanted = [(home + step + NGB) % NGB for step in (-1, 0, 1, 2, NGB // 2)]
    for i in range(TR):
        cond = bk32[i, CR : CR + BLK, :].astype(BF16).astype(F32)
        target = targets_ref[0, i]
        for n in range(5):
            mask = (target == wanted[n]).astype(F32)
            cmask[n * BLK : (n + 1) * BLK, i * TC : (i + 1) * TC] = (cond * mask).astype(BF16)
    pend.pop(4)()
    glob_out[...] = jnp.dot(
        cmask[...], interp_v[...].reshape(TR * TC, TC), preferred_element_type=F32
    ).reshape(5, BLK, TC)
    for n, (block, step) in enumerate(((0, -1), (3, 1), (4, 64))):
        pltpu.make_async_remote_copy(
            glob_out.at[block], glob_recv.at[n], gl_ss.at[0], gl_rs.at[0],
            device_id=flat_dev(step), device_id_type=MESH,
        ).start()
    pend["glob_s"] = bulk(glob_recv, gl_ss.at[0])
    pend["glob"] = bulk(glob_recv, gl_rs.at[0])
    pend.pop("z")()
    full = zbuf[0].astype(F32)
    for n in range(1, 8):
        full = full + zbuf[n].astype(F32)
    gbuf[core, q] = (full * SCALE_NORM).astype(BF16)

    for d in PLANE:
        pltpu.make_async_remote_copy(
            gbuf.at[core, q], gbuf.at[core, q], ag_ss, ag_rs.at[d // 4],
            device_id=plane_dev(d), device_id_type=MESH,
        ).start()
    pend["ag_s"] = bulk(gbuf.at[0, pl.ds(0, 15)], ag_ss)

    pend.pop("glob")()
    own[0] = glob_out[1] + glob_recv[1] + glob_recv[2]
    own[1] = glob_out[2] + glob_recv[0]
    cpl_copy = pltpu.make_async_remote_copy(
        own, cplrecv, gl_ss.at[1], gl_rs.at[1], device_id=other, device_id_type=MESH
    )
    cpl_copy.start()
    pend["cpl_s"] = cpl_copy.wait_send
    pend["cpl"] = cpl_copy.wait_recv

    for dx in (0, 1, 3, 2):
        count = 3 if dx == 0 else 4
        bulk(gbuf.at[0, pl.ds(0, count)], ag_rs.at[dx])()
        column = gbuf.at[core, pl.ds(lax.rem(x + 4 - dx, 4) * 4, 4)]
        pltpu.make_async_remote_copy(
            column, column, fw_ss, fw_rs, device_id=sibling, device_id_type=MESH
        ).start()
    pend["fw_s"] = bulk(gbuf.at[0], fw_ss)
    pend.pop("cpl")()
    ggrad_ref[...] = own[...] + cplrecv[...]
    bulk(gbuf.at[0], fw_rs)()
    for wait in pend.values():
        wait()


def finish(ig_v, gbuf, gg_v, igrad_hbm, wgrad_hbm, bgrad_hbm, ggrad_hbm, w32, b32, g32, sem):
    first = pltpu.make_async_copy(ig_v, igrad_hbm.at[0], sem.at[0])
    first.start()
    for n in range(2):
        g32[:, n : n + 1, :] = gg_v[n, :CG, :].reshape(CG, 1, TC)
    second = pltpu.make_async_copy(g32, ggrad_hbm, sem.at[1])
    second.start()
    for h in range(2):
        for p in range(16):
            part = gbuf[h, p].astype(F32)
            for s in range(PIECE // 8):
                row = p * PIECE + s * 8
                if row >= ROWS_HALF:
                    continue
                k, c = row // HALF, row % HALF + h * HALF
                keep = min(8, CIN - c)
                w32[k, c : c + keep, :] = part[s * 8 : s * 8 + keep]
                if h == 1 and k == 0 and c <= CIN < c + 8:
                    b32[...] = part[s * 8 + CIN - c]

    third = pltpu.make_async_copy(w32, wgrad_hbm, sem.at[2])
    third.start()
    fourth = pltpu.make_async_copy(b32, bgrad_hbm, sem.at[3])
    fourth.start()
    for copy in (first, second, third, fourth):
        copy.wait()


def body(saved_input, pre_act, cotangent, conv_weight, interp, targets, noise_index):
    vmem = pl.BlockSpec(memory_space=pltpu.VMEM)
    smem = pl.BlockSpec(memory_space=pltpu.SMEM)
    hbm = pl.BlockSpec(memory_space=pltpu.HBM)
    dma = pltpu.SemaphoreType.DMA
    pinned = [
        pltpu.with_memory_space_constraint(v, pltpu.HBM)
        for v in (saved_input, pre_act, cotangent, conv_weight, interp, targets)
    ]
    parts = pl.pallas_call(
        kernel,
        out_shape=(
            jax.ShapeDtypeStruct((CR, TR, TC), BF16),
            jax.ShapeDtypeStruct((2, 16, PIECE, CH), BF16),
            jax.ShapeDtypeStruct((2, BLK, TC), F32),
        ),
        in_specs=[hbm] * 6 + [smem],
        out_specs=(vmem, vmem, vmem),
        scratch_shapes=[
            pltpu.VMEM((CIN, TR, TC), BF16),
            pltpu.VMEM((CH, TR, TC), BF16),
            pltpu.VMEM((CH, TR, TC), BF16),
            pltpu.VMEM((9, CIN, CH), BF16),
            pltpu.VMEM((TR, TC, TC), BF16),
            pltpu.SMEM((1, TR), jnp.int32),
            pltpu.VMEM((CH * TR, TC), F32),
            pltpu.VMEM((CPAD * TR, TC), F32),
            pltpu.VMEM((TR + 2, PITCH, CH), F32),
            pltpu.VMEM(((TR + 2) * TC, 3 * CH), BF16),
            pltpu.VMEM((CPAD, TR * TC), BF16),
            pltpu.VMEM((3, CPAD, 3 * CH), BF16),
            pltpu.VMEM((2, TR, CH), F32),
            pltpu.VMEM((2, TR, CH), F32),
            pltpu.VMEM((2, 2, 8, CH), F32),
            pltpu.VMEM((2, CPAD, TC), BF16),
            pltpu.VMEM((2, CPAD, TC), BF16),
            pltpu.VMEM((TR * TC, TC), BF16),
            pltpu.VMEM((CPAD, TC), BF16),
            pltpu.VMEM((2, 24, CH), F32),
            pltpu.VMEM((3, TC, 3 * CH), BF16),
            pltpu.VMEM((2, ROWS_PAD, CH), F32),
            pltpu.VMEM((ROWS_PAD, CH), F32),
            pltpu.VMEM((ROWS_ALL, CH), BF16),
            pltpu.VMEM((16, PIECE, CH), BF16),
            pltpu.VMEM((8, PIECE, CH), BF16),
            pltpu.VMEM((TR, CPAD + 8, TC), F32),
            pltpu.VMEM((5 * BLK, TR * TC), BF16),
            pltpu.VMEM((5, BLK, TC), F32),
            pltpu.VMEM((3, BLK, TC), F32),
            pltpu.VMEM((2, BLK, TC), F32),
            pltpu.VMEM((2, BLK, TC), F32),
            dma((6,)),
            dma((4,)),
            dma((4,)),
            dma,
            dma,
            dma,
            dma,
            dma,
            dma,
            dma,
            dma((4,)),
            dma,
            dma,
            dma((2,)),
            dma((2,)),
        ],
        compiler_params=pltpu.CompilerParams(
            collective_id=0, has_side_effects=True, vmem_limit_bytes=40 << 20
        ),
        cost_estimate=pl.CostEstimate(
            flops=2 * 2 * CIN * 9 * CH * TR * TC, bytes_accessed=4 << 20, transcendentals=CH * TR * TC
        ),
    )(*pinned, noise_index)
    igrad, wgrad, bgrad, ggrad = pl.pallas_call(
        finish,
        out_shape=(
            pltpu.HBM((1, CR, TR, TC), BF16),
            pltpu.HBM((9, CIN, CH), F32),
            pltpu.HBM((CH,), F32),
            pltpu.HBM((CG, 2, TC), F32),
        ),
        in_specs=[vmem] * 3,
        out_specs=(hbm, hbm, hbm, hbm),
        scratch_shapes=[
            pltpu.VMEM((9, CIN, CH), F32),
            pltpu.VMEM((CH,), F32),
            pltpu.VMEM((CG, 2, TC), F32),
            dma((4,)),
        ],
        compiler_params=pltpu.CompilerParams(vmem_limit_bytes=16 << 20),
    )(*parts)
    return igrad, wgrad, bgrad, jnp.transpose(ggrad, (1, 0, 2))


def solution(mesh):
    in_specs = (
        P("cpl", None, "reg", "glob"),
        P("cpl", None, "reg", "glob"),
        P("cpl", None, "reg", "glob"),
        P(),
        P("glob", "reg", None, None),
        P("glob", "reg"),
        P("cpl"),
    )
    out_specs = (P("cpl", None, "reg", "glob"), P(), P(), P(("reg", "glob"), None, None))
    return jax.shard_map(body, mesh=mesh, in_specs=in_specs, out_specs=out_specs, check_vma=False)
```

```python
import math

import jax
import jax.numpy as jnp
from jax import lax
from jax.experimental import pallas as pl
from jax.experimental.pallas import tpu as pltpu
from jax.sharding import PartitionSpec as P

CH = 128
CR = 99
CG = 73
CIN = 172
CPAD = 176
HALF = 88
TR = 16
TC = 128
NGB = 256
NOISE_LEVELS = 18
PIECE = 64
ROWS_HALF = 9 * HALF
ROWS_PAD = 800
ROWS_ALL = 16 * PIECE
TOP = 8
PITCH = TOP + TC + 8
BLK = 80
SCALE_NORM = 1.0 / math.sqrt(512 * 512 * 2)
PLANE = (10, 9, 11, 6, 14, 8, 2, 5, 7, 13, 15, 4, 12, 1, 3)
ZLINE = (4, 3, 5, 2, 6, 1, 7)
MESH = pl.DeviceIdType.MESH
F32 = jnp.float32
BF16 = jnp.bfloat16


def kernel(
    saved_hbm, pre_hbm, cot_hbm, w_hbm, interp_hbm, targets_hbm, noise_ref,
    ig_v, gbuf, ggrad_ref,
    saved_v, pre_v, cot_v, w_v, interp_v, targets_ref,
    d32, s32, p32, dzc, smat, wcat, colbuf, colrecv, corner,
    rows_out, rows_in, pick, edge, lpad, extra,
    awh, crecv, acc, xrecv, zbuf,
    bk32, cmask, glob_out, glob_recv, own, cplrecv,
    in_sem, halo_ss, halo_rs, core_ss, core_rs, xy_ss, xy_rs, z_ss, z_rs,
    ag_ss, ag_rs, fw_ss, fw_rs, gl_ss, gl_rs,
):
    reg = lax.axis_index("reg")
    glob = lax.axis_index("glob")
    cpl = lax.axis_index("cpl")
    z = reg // 4
    x_lo = (reg // 2) % 2
    core = reg % 2
    x = cpl * 2 + x_lo
    y = glob
    q = x * 4 + y

    def at(x_, y_, z_, core_):
        return {"reg": z_ * 4 + (x_ % 2) * 2 + core_, "glob": y_, "cpl": x_ // 2}

    def plane(d):
        return (x + d // 4) % 4, (y + d % 4) % 4

    def plane_dev(d):
        px, py = plane(d)
        return at(px, py, z, core)

    def z_dev(d):
        return at(x, y, (z + d) % 8, core)

    def halo_dev(dr, dg):
        return {"reg": (reg + dr + 32) % 32, "glob": (glob + dg + 4) % 4, "cpl": cpl}

    def flat_dev(step):
        flat = (reg * 4 + glob + step + 128) % 128
        return {"reg": flat // 4, "glob": flat % 4, "cpl": cpl}

    sibling = at(x, y, z, 1 - core)
    other = {"reg": reg, "glob": glob, "cpl": 1 - cpl}

    loads = [
        pltpu.make_async_copy(src, dst, in_sem.at[n])
        for n, (src, dst) in enumerate((
            (pre_hbm.at[0], pre_v),
            (cot_hbm.at[0], cot_v),
            (saved_hbm.at[0], saved_v),
            (w_hbm, w_v),
            (interp_hbm.at[0], interp_v),
            (targets_hbm, targets_ref),
        ))
    ]
    barrier = pltpu.get_barrier_semaphore()

    def greet(device):
        pl.semaphore_signal(barrier, inc=1, device_id=device, device_id_type=MESH)

    halo_steps = [(dr, dg) for dr in (-1, 0, 1) for dg in (-1, 0, 1) if dr or dg]
    greet(flat_dev(64))
    for d in ZLINE:
        greet(z_dev(d))
    for load in loads:
        load.start()
    pend = {n: load.wait for n, load in enumerate(loads)}

    for d in PLANE:
        greet(plane_dev(d))
    for dr, dg in halo_steps:
        greet(halo_dev(dr, dg))
    for step in (-1, 1):
        greet(flat_dev(step))
    greet(other)
    greet(sibling)

    s32[CIN * TR :, :] = jnp.zeros((CPAD * TR - CIN * TR, TC), F32)
    wcat[:, CPAD - 16 :, :] = jnp.zeros((3, 16, 3 * CH), BF16)
    acc[ROWS_PAD:, :] = jnp.zeros((ROWS_ALL - ROWS_PAD, CH), BF16)
    awh[:, ROWS_HALF:, :] = jnp.zeros((2, ROWS_PAD - ROWS_HALF, CH), F32)
    crecv[ROWS_HALF:, :] = jnp.zeros((ROWS_PAD - ROWS_HALF, CH), F32)
    for i in range(TR):
        p32[i + 1, :TOP, :] = jnp.zeros((TOP, CH), F32)
        p32[i + 1, TOP + TC :, :] = jnp.zeros((8, CH), F32)
    lpad[...] = jnp.zeros((2, 24, CH), F32)
    extra[...] = jnp.zeros((3, TC, 3 * CH), BF16)
    bk32[:, CPAD:, :] = jnp.zeros((TR, 8, TC), F32)

    pend.pop(0)()
    pend.pop(1)()

    def silu_step(n, carry):
        pre = pre_v[pl.ds(n * 8, 8)].astype(F32)
        cot = cot_v[pl.ds(n * 8, 8)].astype(F32)
        sig = 0.5 * jnp.tanh(0.5 * pre) + 0.5
        dz = cot * sig * (1.0 + pre * (1.0 - sig))
        d32[pl.ds(pl.multiple_of(n * 8 * TR, 128), 8 * TR), :] = dz.reshape(8 * TR, TC)
        return carry

    lax.fori_loop(0, CH // 8, silu_step, 0)

    def turn(i):
        tile = jnp.transpose(d32[pl.ds(i, CH, stride=TR), :], (1, 0))
        p32[i + 1, TOP : TOP + TC, :] = tile
        colbuf[0, i : i + 1, :] = tile[:1]
        colbuf[1, i : i + 1, :] = tile[TC - 1 :]
        return tile

    total = jnp.zeros((TC, CH), F32)
    for i in range(TR):
        total = total + turn(i)
    bias = jnp.sum(total, axis=0, keepdims=True)

    pend.pop(2)()

    def saved_step(n, carry):
        part = saved_v[pl.ds(n * 4, 4)].astype(F32)
        s32[pl.ds(pl.multiple_of(n * 4 * TR, 64), 4 * TR), :] = part.reshape(4 * TR, TC)
        return carry

    lax.fori_loop(0, CIN // 4, saved_step, 0)
    rows_out[0] = s32[pl.ds(0, CPAD, stride=TR), :].astype(BF16)
    rows_out[1] = s32[pl.ds(TR - 1, CPAD, stride=TR), :].astype(BF16)

    pl.semaphore_wait(barrier, 8 + 3 + 1 + 1 + 15 + 7)

    def send(src, dst, kind, dr, dg):
        pltpu.make_async_remote_copy(
            src, dst, halo_ss.at[kind], halo_rs.at[kind],
            device_id=halo_dev(dr, dg), device_id_type=MESH,
        ).start()

    def bulk(ref, sem):
        return pltpu.make_async_copy(ref, ref, sem).wait

    send(rows_out.at[0], rows_in.at[1], 0, -1, 0)
    send(rows_out.at[1], rows_in.at[0], 0, 1, 0)
    send(colbuf.at[0], colrecv.at[1], 1, 0, -1)
    send(colbuf.at[1], colrecv.at[0], 1, 0, 1)
    halo_bulk = (rows_in, colrecv, d32.at[pl.ds(0, 2 * TC)], corner)
    for kind in range(4):
        pend["halo_s", kind] = bulk(halo_bulk[kind], halo_ss.at[kind])
        pend["halo", kind] = bulk(halo_bulk[kind], halo_rs.at[kind])

    for i in range(TR):
        smat[:, i * TC : (i + 1) * TC] = s32[pl.ds(i, CPAD, stride=TR), :].astype(BF16)

    def shift_rows(i):
        for bi in range(3):
            dzc[pl.ds(pl.multiple_of(i * TC, TC), TC), bi * CH : (bi + 1) * CH] = p32[
                i, TOP + 1 - bi : TOP + 1 - bi + TC, :
            ].astype(BF16)

    lax.fori_loop(1, TR + 1, lambda i, c: (shift_rows(i), c)[1], 0)
    for a in range(3):
        first, count = max(a - 1, 0), TR - abs(a - 1)
        start = TC * (first + 2 - a)
        term = jnp.dot(
            smat[:, first * TC : (first + count) * TC], dzc[start : start + count * TC, :],
            preferred_element_type=F32,
        )
        for bi in range(3):
            k = 3 * a + bi
            for h in range(2):
                awh[h, k * HALF : (k + 1) * HALF, :] = term[
                    h * HALF : (h + 1) * HALF, bi * CH : (bi + 1) * CH
                ]

    for dr, dg in halo_steps:
        row = TR if dr > 0 else 1
        if dg == 0:
            dst = p32.at[0 if dr > 0 else TR + 1, pl.ds(TOP, TC)]
            send(p32.at[row, pl.ds(TOP, TC)], dst, 2, dr, dg)
        elif dr != 0:
            dst = corner.at[0 if dr > 0 else 1, 0 if dg > 0 else 1]
            send(p32.at[row, pl.ds(TOP + TC - 8 if dg > 0 else TOP, 8)], dst, 3, dr, dg)

    at_row = lax.broadcasted_iota(jnp.int32, (TC, TC), 0)
    at_lane = lax.broadcasted_iota(jnp.int32, (TC, TC), 1)
    for i in range(TR):
        first = (at_row == 0) & (at_lane == i)
        last = (at_row == TC - 1) & (at_lane == TR + i)
        pick[i * TC : (i + 1) * TC, :] = jnp.where(first | last, 1.0, 0.0).astype(BF16)
    edge[...] = jnp.dot(smat[...], pick[...], preferred_element_type=F32).astype(BF16)

    pend.pop(("halo", 0))()
    pend.pop(("halo", 1))()
    up = (reg > 0).astype(F32)
    down = (reg < 31).astype(F32)
    left = (glob > 0).astype(F32)
    right = (glob < 3).astype(F32)
    lpad[0, 1 : TR + 1, :] = colrecv[0] * left
    lpad[1, 1 : TR + 1, :] = colrecv[1] * right
    for i in range(TR):
        p32[i + 1, TOP - 1 : TOP, :] = lpad[0, i + 1 : i + 2, :]
        p32[i + 1, TOP + TC : TOP + TC + 1, :] = lpad[1, i + 1 : i + 2, :]
    shift_rows(1)
    shift_rows(TR)
    for a in range(3):
        extra[a, :TR, 2 * CH :] = lpad[0, 2 - a : 2 - a + TR, :].astype(BF16)
        extra[a, TR : 2 * TR, :CH] = lpad[1, 2 - a : 2 - a + TR, :].astype(BF16)

    for a in range(3):
        term = jnp.dot(edge[...], extra[a], preferred_element_type=F32)
        if a == 0:
            term = term + up * jnp.dot(
                rows_in[0], dzc[TC : 2 * TC, :], preferred_element_type=F32
            )
        if a == 2:
            term = term + down * jnp.dot(
                rows_in[1], dzc[TR * TC : (TR + 1) * TC, :], preferred_element_type=F32
            )
        for bi in range(3):
            k = 3 * a + bi
            for h in range(2):
                rows = slice(k * HALF, (k + 1) * HALF)
                awh[h, rows, :] = awh[h, rows, :] + term[
                    h * HALF : (h + 1) * HALF, bi * CH : (bi + 1) * CH
                ]
        if a == 0:
            awh[1, CIN - HALF : CIN - HALF + 1, :] = bias
        rows = pl.ds(3 * a * HALF, 3 * HALF)
        pltpu.make_async_remote_copy(
            awh.at[1 - core, rows], crecv.at[rows], core_ss, core_rs,
            device_id=sibling, device_id_type=MESH,
        ).start()
    pend["core_s"] = bulk(crecv.at[pl.ds(0, ROWS_HALF)], core_ss)
    pend["core"] = bulk(crecv.at[pl.ds(0, ROWS_HALF)], core_rs)
    pend.pop("core")()
    acc[:ROWS_PAD, :] = (awh[core] + crecv[...]).astype(BF16)
    for d in PLANE:
        px, py = plane(d)
        pltpu.make_async_remote_copy(
            acc.at[pl.ds(pl.multiple_of((px * 4 + py) * PIECE, PIECE), PIECE)],
            xrecv.at[d], xy_ss, xy_rs,
            device_id=at(px, py, z, core), device_id_type=MESH,
        ).start()
    pend["xy_s"] = bulk(xrecv.at[pl.ds(1, 15)], xy_ss)
    pend["xy"] = bulk(xrecv.at[pl.ds(1, 15)], xy_rs)
    pend.pop(3)()
    for a in range(3):
        for bi in range(3):
            wcat[a, :CIN, bi * CH : (bi + 1) * CH] = w_v[3 * a + bi]
    lax.fori_loop(2, TR, lambda i, c: (shift_rows(i), c)[1], 0)

    level = jnp.full((1, TC), noise_ref[0], jnp.int32).astype(F32) / (NOISE_LEVELS - 1)
    sigma = jnp.exp(math.log(2.0) + level * (math.log(0.05) - math.log(2.0)))
    scale = 1.0 / jnp.sqrt(sigma * sigma + 0.25)

    def back_step(n, carry):
        back = jnp.zeros((CPAD, 2 * TC), F32)
        for a in range(3):
            start = pl.multiple_of((2 * n + 2 - a) * TC, TC)
            back = back + lax.dot_general(
                wcat[a], dzc[pl.ds(start, 2 * TC), :], (((1,), (1,)), ((), ())),
                preferred_element_type=F32,
            )
        for half in range(2):
            part = back[:, half * TC : (half + 1) * TC]
            bk32[2 * n + half, :CPAD, :] = part
            d32[pl.ds(2 * n + half, CR, stride=TR), :] = part[:CR] * scale
        return carry

    lax.fori_loop(1, TR // 2 - 1, back_step, 0)

    pend.pop("xy")()
    piece = acc[pl.ds(pl.multiple_of(q * PIECE, PIECE), PIECE), :].astype(F32)
    for d in range(1, 16):
        piece = piece + xrecv[d].astype(F32)
    zbuf[z] = piece.astype(BF16)

    for d in ZLINE:
        pltpu.make_async_remote_copy(
            zbuf.at[z], zbuf.at[z], z_ss, z_rs, device_id=z_dev(d), device_id_type=MESH
        ).start()
    pend["z_s"] = bulk(zbuf.at[pl.ds(0, 7)], z_ss)
    pend["z"] = bulk(zbuf.at[pl.ds(0, 7)], z_rs)

    pend.pop(("halo", 2))()
    pend.pop(("halo", 3))()
    p32[0, TOP : TOP + TC, :] = p32[0, TOP : TOP + TC, :] * up
    p32[TR + 1, TOP : TOP + TC, :] = p32[TR + 1, TOP : TOP + TC, :] * down
    p32[0, TOP - 1 : TOP, :] = corner[0, 0, 7:8, :] * (up * left)
    p32[0, TOP + TC : TOP + TC + 1, :] = corner[0, 1, 0:1, :] * (up * right)
    p32[TR + 1, TOP - 1 : TOP, :] = corner[1, 0, 7:8, :] * (down * left)
    p32[TR + 1, TOP + TC : TOP + TC + 1, :] = corner[1, 1, 0:1, :] * (down * right)
    shift_rows(0)
    shift_rows(TR + 1)

    back_step(0, 0)
    back_step(TR // 2 - 1, 0)

    def igrad_step(n, carry):
        rows = d32[pl.ds(pl.multiple_of(n * 9 * TR, 16), 9 * TR), :]
        ig_v[pl.ds(n * 9, 9)] = rows.reshape(9, TR, TC).astype(BF16)
        return carry

    lax.fori_loop(0, CR // 9, igrad_step, 0)
    pend.pop(5)()
    home = (reg * 4 + glob) * 2
    wanted = [(home + step + NGB) % NGB for step in (-1, 0, 1, 2, NGB // 2)]
    for i in range(TR):
        cond = bk32[i, CR : CR + BLK, :].astype(BF16).astype(F32)
        target = targets_ref[0, i]
        for n in range(5):
            mask = (target == wanted[n]).astype(F32)
            cmask[n * BLK : (n + 1) * BLK, i * TC : (i + 1) * TC] = (cond * mask).astype(BF16)
    pend.pop(4)()
    glob_out[...] = jnp.dot(
        cmask[...], interp_v[...].reshape(TR * TC, TC), preferred_element_type=F32
    ).reshape(5, BLK, TC)
    for n, (block, step) in enumerate(((0, -1), (3, 1), (4, 64))):
        pltpu.make_async_remote_copy(
            glob_out.at[block], glob_recv.at[n], gl_ss.at[0], gl_rs.at[0],
            device_id=flat_dev(step), device_id_type=MESH,
        ).start()
    pend["glob_s"] = bulk(glob_recv, gl_ss.at[0])
    pend["glob"] = bulk(glob_recv, gl_rs.at[0])
    pend.pop("z")()
    full = zbuf[0].astype(F32)
    for n in range(1, 8):
        full = full + zbuf[n].astype(F32)
    gbuf[core, q] = (full * SCALE_NORM).astype(BF16)

    for d in PLANE:
        pltpu.make_async_remote_copy(
            gbuf.at[core, q], gbuf.at[core, q], ag_ss, ag_rs.at[d // 4],
            device_id=plane_dev(d), device_id_type=MESH,
        ).start()
    pend["ag_s"] = bulk(gbuf.at[0, pl.ds(0, 15)], ag_ss)

    pend.pop("glob")()
    own[0] = glob_out[1] + glob_recv[1] + glob_recv[2]
    own[1] = glob_out[2] + glob_recv[0]
    cpl_copy = pltpu.make_async_remote_copy(
        own, cplrecv, gl_ss.at[1], gl_rs.at[1], device_id=other, device_id_type=MESH
    )
    cpl_copy.start()
    pend["cpl_s"] = cpl_copy.wait_send
    pend["cpl"] = cpl_copy.wait_recv

    for dx in (0, 1, 3, 2):
        count = 3 if dx == 0 else 4
        bulk(gbuf.at[0, pl.ds(0, count)], ag_rs.at[dx])()
        column = gbuf.at[core, pl.ds(lax.rem(x + 4 - dx, 4) * 4, 4)]
        pltpu.make_async_remote_copy(
            column, column, fw_ss, fw_rs, device_id=sibling, device_id_type=MESH
        ).start()
    pend["fw_s"] = bulk(gbuf.at[0], fw_ss)
    pend.pop("cpl")()
    ggrad_ref[...] = own[...] + cplrecv[...]
    bulk(gbuf.at[0], fw_rs)()
    for wait in pend.values():
        wait()


def finish(ig_v, gbuf, gg_v, igrad_hbm, wgrad_hbm, bgrad_hbm, ggrad_hbm, w32, b32, g32, sem):
    first = pltpu.make_async_copy(ig_v, igrad_hbm.at[0], sem.at[0])
    first.start()
    for n in range(2):
        g32[:, n : n + 1, :] = gg_v[n, :CG, :].reshape(CG, 1, TC)
    second = pltpu.make_async_copy(g32, ggrad_hbm, sem.at[1])
    second.start()
    for h in range(2):
        for p in range(16):
            part = gbuf[h, p].astype(F32)
            for s in range(PIECE // 8):
                row = p * PIECE + s * 8
                if row >= ROWS_HALF:
                    continue
                k, c = row // HALF, row % HALF + h * HALF
                keep = min(8, CIN - c)
                w32[k, c : c + keep, :] = part[s * 8 : s * 8 + keep]
                if h == 1 and k == 0 and c <= CIN < c + 8:
                    b32[...] = part[s * 8 + CIN - c]

    third = pltpu.make_async_copy(w32, wgrad_hbm, sem.at[2])
    third.start()
    fourth = pltpu.make_async_copy(b32, bgrad_hbm, sem.at[3])
    fourth.start()
    for copy in (first, second, third, fourth):
        copy.wait()


def body(saved_input, pre_act, cotangent, conv_weight, interp, targets, noise_index):
    vmem = pl.BlockSpec(memory_space=pltpu.VMEM)
    smem = pl.BlockSpec(memory_space=pltpu.SMEM)
    hbm = pl.BlockSpec(memory_space=pltpu.HBM)
    dma = pltpu.SemaphoreType.DMA
    pinned = [
        pltpu.with_memory_space_constraint(v, pltpu.HBM)
        for v in (saved_input, pre_act, cotangent, conv_weight, interp, targets)
    ]
    parts = pl.pallas_call(
        kernel,
        out_shape=(
            jax.ShapeDtypeStruct((CR, TR, TC), BF16),
            jax.ShapeDtypeStruct((2, 16, PIECE, CH), BF16),
            jax.ShapeDtypeStruct((2, BLK, TC), F32),
        ),
        in_specs=[hbm] * 6 + [smem],
        out_specs=(vmem, vmem, vmem),
        scratch_shapes=[
            pltpu.VMEM((CIN, TR, TC), BF16),
            pltpu.VMEM((CH, TR, TC), BF16),
            pltpu.VMEM((CH, TR, TC), BF16),
            pltpu.VMEM((9, CIN, CH), BF16),
            pltpu.VMEM((TR, TC, TC), BF16),
            pltpu.SMEM((1, TR), jnp.int32),
            pltpu.VMEM((CH * TR, TC), F32),
            pltpu.VMEM((CPAD * TR, TC), F32),
            pltpu.VMEM((TR + 2, PITCH, CH), F32),
            pltpu.VMEM(((TR + 2) * TC, 3 * CH), BF16),
            pltpu.VMEM((CPAD, TR * TC), BF16),
            pltpu.VMEM((3, CPAD, 3 * CH), BF16),
            pltpu.VMEM((2, TR, CH), F32),
            pltpu.VMEM((2, TR, CH), F32),
            pltpu.VMEM((2, 2, 8, CH), F32),
            pltpu.VMEM((2, CPAD, TC), BF16),
            pltpu.VMEM((2, CPAD, TC), BF16),
            pltpu.VMEM((TR * TC, TC), BF16),
            pltpu.VMEM((CPAD, TC), BF16),
            pltpu.VMEM((2, 24, CH), F32),
            pltpu.VMEM((3, TC, 3 * CH), BF16),
            pltpu.VMEM((2, ROWS_PAD, CH), F32),
            pltpu.VMEM((ROWS_PAD, CH), F32),
            pltpu.VMEM((ROWS_ALL, CH), BF16),
            pltpu.VMEM((16, PIECE, CH), BF16),
            pltpu.VMEM((8, PIECE, CH), BF16),
            pltpu.VMEM((TR, CPAD + 8, TC), F32),
            pltpu.VMEM((5 * BLK, TR * TC), BF16),
            pltpu.VMEM((5, BLK, TC), F32),
            pltpu.VMEM((3, BLK, TC), F32),
            pltpu.VMEM((2, BLK, TC), F32),
            pltpu.VMEM((2, BLK, TC), F32),
            dma((6,)),
            dma((4,)),
            dma((4,)),
            dma,
            dma,
            dma,
            dma,
            dma,
            dma,
            dma,
            dma((4,)),
            dma,
            dma,
            dma((2,)),
            dma((2,)),
        ],
        compiler_params=pltpu.CompilerParams(
            collective_id=0, has_side_effects=True, vmem_limit_bytes=40 << 20
        ),
        cost_estimate=pl.CostEstimate(
            flops=2 * 2 * CIN * 9 * CH * TR * TC, bytes_accessed=4 << 20, transcendentals=CH * TR * TC
        ),
    )(*pinned, noise_index)
    igrad, wgrad, bgrad, ggrad = pl.pallas_call(
        finish,
        out_shape=(
            pltpu.HBM((1, CR, TR, TC), BF16),
            pltpu.HBM((9, CIN, CH), F32),
            pltpu.HBM((CH,), F32),
            pltpu.HBM((CG, 2, TC), F32),
        ),
        in_specs=[vmem] * 3,
        out_specs=(hbm, hbm, hbm, hbm),
        scratch_shapes=[
            pltpu.VMEM((9, CIN, CH), F32),
            pltpu.VMEM((CH,), F32),
            pltpu.VMEM((CG, 2, TC), F32),
            dma((4,)),
        ],
        compiler_params=pltpu.CompilerParams(vmem_limit_bytes=16 << 20),
    )(*parts)
    return igrad, wgrad, bgrad, jnp.transpose(ggrad, (1, 0, 2))


def solution(mesh):
    in_specs = (
        P("cpl", None, "reg", "glob"),
        P("cpl", None, "reg", "glob"),
        P("cpl", None, "reg", "glob"),
        P(),
        P("glob", "reg", None, None),
        P("glob", "reg"),
        P("cpl"),
    )
    out_specs = (P("cpl", None, "reg", "glob"), P(), P(), P(("reg", "glob"), None, None))
    return jax.shard_map(body, mesh=mesh, in_specs=in_specs, out_specs=out_specs, check_vma=False)
```

```python
import math

import jax
import jax.numpy as jnp
from jax import lax
from jax.experimental import pallas as pl
from jax.experimental.pallas import tpu as pltpu
from jax.sharding import PartitionSpec as P

CH = 128
CR = 99
CG = 73
CIN = 172
CPAD = 176
HALF = 88
TR = 16
TC = 128
NGB = 256
NOISE_LEVELS = 18
PIECE = 64
ROWS_HALF = 9 * HALF
ROWS_PAD = 800
ROWS_ALL = 16 * PIECE
TOP = 8
PITCH = TOP + TC + 8
BLK = 80
SCALE_NORM = 1.0 / math.sqrt(512 * 512 * 2)
PLANE = (10, 9, 11, 6, 14, 8, 2, 5, 7, 13, 15, 4, 12, 1, 3)
ZLINE = (4, 3, 5, 2, 6, 1, 7)
MESH = pl.DeviceIdType.MESH
F32 = jnp.float32
BF16 = jnp.bfloat16


def kernel(
    saved_hbm, pre_hbm, cot_hbm, w_hbm, interp_hbm, targets_hbm, noise_ref,
    ig_v, gbuf, ggrad_ref,
    saved_v, pre_v, cot_v, w_v, interp_v, targets_ref,
    d32, s32, p32, dzc, smat, wcat, colbuf, colrecv, corner,
    rows_out, sides, pick, lpad, extra,
    awh, crecv, acc, xrecv, zbuf,
    bk32, cmask, glob_out, glob_recv, own, cplrecv,
    in_sem, halo_ss, halo_rs, core_ss, core_rs, xy_ss, xy_rs, z_ss, z_rs,
    ag_ss, ag_rs, fw_ss, fw_rs, gl_ss, gl_rs,
):
    reg = lax.axis_index("reg")
    glob = lax.axis_index("glob")
    cpl = lax.axis_index("cpl")
    z = reg // 4
    x_lo = (reg // 2) % 2
    core = reg % 2
    x = cpl * 2 + x_lo
    y = glob
    q = x * 4 + y

    def at(x_, y_, z_, core_):
        return {"reg": z_ * 4 + (x_ % 2) * 2 + core_, "glob": y_, "cpl": x_ // 2}

    def plane(d):
        return (x + d // 4) % 4, (y + d % 4) % 4

    def plane_dev(d):
        px, py = plane(d)
        return at(px, py, z, core)

    def z_dev(d):
        return at(x, y, (z + d) % 8, core)

    def halo_dev(dr, dg):
        return {"reg": (reg + dr + 32) % 32, "glob": (glob + dg + 4) % 4, "cpl": cpl}

    def flat_dev(step):
        flat = (reg * 4 + glob + step + 128) % 128
        return {"reg": flat // 4, "glob": flat % 4, "cpl": cpl}

    sibling = at(x, y, z, 1 - core)
    other = {"reg": reg, "glob": glob, "cpl": 1 - cpl}

    loads = [
        pltpu.make_async_copy(src, dst, in_sem.at[n])
        for n, (src, dst) in enumerate((
            (pre_hbm.at[0], pre_v),
            (cot_hbm.at[0], cot_v),
            (saved_hbm.at[0], saved_v),
            (w_hbm, w_v),
            (interp_hbm.at[0], interp_v),
            (targets_hbm, targets_ref),
        ))
    ]
    barrier = pltpu.get_barrier_semaphore()

    def greet(device):
        pl.semaphore_signal(barrier, inc=1, device_id=device, device_id_type=MESH)

    halo_steps = [(dr, dg) for dr in (-1, 0, 1) for dg in (-1, 0, 1) if dr or dg]
    greet(flat_dev(64))
    for d in ZLINE:
        greet(z_dev(d))
    for load in loads:
        load.start()
    pend = {n: load.wait for n, load in enumerate(loads)}

    for d in PLANE:
        greet(plane_dev(d))
    for dr, dg in halo_steps:
        greet(halo_dev(dr, dg))
    for step in (-1, 1):
        greet(flat_dev(step))
    greet(other)
    greet(sibling)

    s32[CIN * TR :, :] = jnp.zeros((CPAD * TR - CIN * TR, TC), F32)
    wcat[:, CPAD - 16 :, :] = jnp.zeros((3, 16, 3 * CH), BF16)
    acc[ROWS_PAD:, :] = jnp.zeros((ROWS_ALL - ROWS_PAD, CH), BF16)
    awh[:, ROWS_HALF:, :] = jnp.zeros((2, ROWS_PAD - ROWS_HALF, CH), F32)
    crecv[ROWS_HALF:, :] = jnp.zeros((ROWS_PAD - ROWS_HALF, CH), F32)
    for i in range(TR):
        p32[i + 1, :TOP, :] = jnp.zeros((TOP, CH), F32)
        p32[i + 1, TOP + TC :, :] = jnp.zeros((8, CH), F32)
    lpad[...] = jnp.zeros((2, 24, CH), F32)
    extra[:, :TC, :] = jnp.zeros((3, TC, 3 * CH), BF16)
    bk32[:, CPAD:, :] = jnp.zeros((TR, 8, TC), F32)

    pend.pop(0)()
    pend.pop(1)()

    def silu_step(n, carry):
        pre = pre_v[pl.ds(n * 8, 8)].astype(F32)
        cot = cot_v[pl.ds(n * 8, 8)].astype(F32)
        sig = 0.5 * jnp.tanh(0.5 * pre) + 0.5
        dz = cot * sig * (1.0 + pre * (1.0 - sig))
        d32[pl.ds(pl.multiple_of(n * 8 * TR, 128), 8 * TR), :] = dz.reshape(8 * TR, TC)
        return carry

    lax.fori_loop(0, CH // 8, silu_step, 0)

    def turn(i):
        tile = jnp.transpose(d32[pl.ds(i, CH, stride=TR), :], (1, 0))
        p32[i + 1, TOP : TOP + TC, :] = tile
        colbuf[0, i : i + 1, :] = tile[:1]
        colbuf[1, i : i + 1, :] = tile[TC - 1 :]
        return tile

    total = jnp.zeros((TC, CH), F32)
    for i in range(TR):
        total = total + turn(i)
    bias = jnp.sum(total, axis=0, keepdims=True)

    pend.pop(2)()

    def saved_step(n, carry):
        part = saved_v[pl.ds(n * 4, 4)].astype(F32)
        s32[pl.ds(pl.multiple_of(n * 4 * TR, 64), 4 * TR), :] = part.reshape(4 * TR, TC)
        return carry

    lax.fori_loop(0, CIN // 4, saved_step, 0)
    rows_out[0] = s32[pl.ds(0, CPAD, stride=TR), :].astype(BF16)
    rows_out[1] = s32[pl.ds(TR - 1, CPAD, stride=TR), :].astype(BF16)

    pl.semaphore_wait(barrier, 8 + 3 + 1 + 1 + 15 + 7)

    def send(src, dst, kind, dr, dg):
        pltpu.make_async_remote_copy(
            src, dst, halo_ss.at[kind], halo_rs.at[kind],
            device_id=halo_dev(dr, dg), device_id_type=MESH,
        ).start()

    def bulk(ref, sem):
        return pltpu.make_async_copy(ref, ref, sem).wait

    send(rows_out.at[0], sides.at[2, :, pl.ds(TC, TC)], 0, -1, 0)
    send(rows_out.at[1], sides.at[0, :, pl.ds(TC, TC)], 0, 1, 0)
    send(colbuf.at[0], colrecv.at[1], 1, 0, -1)
    send(colbuf.at[1], colrecv.at[0], 1, 0, 1)
    halo_bulk = (rows_out, colrecv, d32.at[pl.ds(0, 2 * TC)], corner)
    for kind in range(4):
        pend["halo_s", kind] = bulk(halo_bulk[kind], halo_ss.at[kind])
        pend["halo", kind] = bulk(halo_bulk[kind], halo_rs.at[kind])

    for i in range(TR):
        smat[:, i * TC : (i + 1) * TC] = s32[pl.ds(i, CPAD, stride=TR), :].astype(BF16)

    def shift_rows(i):
        for bi in range(3):
            dzc[pl.ds(pl.multiple_of(i * TC, TC), TC), bi * CH : (bi + 1) * CH] = p32[
                i, TOP + 1 - bi : TOP + 1 - bi + TC, :
            ].astype(BF16)

    lax.fori_loop(1, TR + 1, lambda i, c: (shift_rows(i), c)[1], 0)
    for a in range(3):
        first, count = max(a - 1, 0), TR - abs(a - 1)
        start = TC * (first + 2 - a)
        term = jnp.dot(
            smat[:, first * TC : (first + count) * TC], dzc[start : start + count * TC, :],
            preferred_element_type=F32,
        )
        for bi in range(3):
            k = 3 * a + bi
            for h in range(2):
                awh[h, k * HALF : (k + 1) * HALF, :] = term[
                    h * HALF : (h + 1) * HALF, bi * CH : (bi + 1) * CH
                ]

    for dr, dg in halo_steps:
        row = TR if dr > 0 else 1
        if dg == 0:
            dst = p32.at[0 if dr > 0 else TR + 1, pl.ds(TOP, TC)]
            send(p32.at[row, pl.ds(TOP, TC)], dst, 2, dr, dg)
        elif dr != 0:
            dst = corner.at[0 if dr > 0 else 1, 0 if dg > 0 else 1]
            send(p32.at[row, pl.ds(TOP + TC - 8 if dg > 0 else TOP, 8)], dst, 3, dr, dg)

    at_row = lax.broadcasted_iota(jnp.int32, (TC, TC), 0)
    at_lane = lax.broadcasted_iota(jnp.int32, (TC, TC), 1)
    for i in range(TR):
        first = (at_row == 0) & (at_lane == i)
        last = (at_row == TC - 1) & (at_lane == TR + i)
        pick[i * TC : (i + 1) * TC, :] = jnp.where(first | last, 1.0, 0.0).astype(BF16)
    edge = jnp.dot(smat[...], pick[...], preferred_element_type=F32).astype(BF16)
    for a in range(3):
        sides[a, :, :TC] = edge

    pend.pop(3)()
    for a in range(3):
        for bi in range(3):
            wcat[a, :CIN, bi * CH : (bi + 1) * CH] = w_v[3 * a + bi]

    pend.pop(("halo", 0))()
    pend.pop(("halo", 1))()
    up = (reg > 0).astype(F32)
    down = (reg < 31).astype(F32)
    left = (glob > 0).astype(F32)
    right = (glob < 3).astype(F32)
    lpad[0, 1 : TR + 1, :] = colrecv[0] * left
    lpad[1, 1 : TR + 1, :] = colrecv[1] * right
    for i in range(TR):
        p32[i + 1, TOP - 1 : TOP, :] = lpad[0, i + 1 : i + 2, :]
        p32[i + 1, TOP + TC : TOP + TC + 1, :] = lpad[1, i + 1 : i + 2, :]
    for a, row, there in ((0, 1, up), (2, TR, down)):
        for bi in range(3):
            extra[a, TC:, bi * CH : (bi + 1) * CH] = (
                there * p32[row, TOP + 1 - bi : TOP + 1 - bi + TC, :]
            ).astype(BF16)
    for a in range(3):
        extra[a, :TR, 2 * CH :] = lpad[0, 2 - a : 2 - a + TR, :].astype(BF16)
        extra[a, TR : 2 * TR, :CH] = lpad[1, 2 - a : 2 - a + TR, :].astype(BF16)

    for a in (1, 0, 2):
        depth = TC if a == 1 else 2 * TC
        term = jnp.dot(
            sides[a, :, :depth], extra[a, :depth, :], preferred_element_type=F32
        )
        for bi in range(3):
            k = 3 * a + bi
            for h in range(2):
                rows = slice(k * HALF, (k + 1) * HALF)
                awh[h, rows, :] = awh[h, rows, :] + term[
                    h * HALF : (h + 1) * HALF, bi * CH : (bi + 1) * CH
                ]
        if a == 0:
            awh[1, CIN - HALF : CIN - HALF + 1, :] = bias
        rows = pl.ds(3 * a * HALF, 3 * HALF)
        pltpu.make_async_remote_copy(
            awh.at[1 - core, rows], crecv.at[rows], core_ss, core_rs,
            device_id=sibling, device_id_type=MESH,
        ).start()
    pend["core_s"] = bulk(crecv.at[pl.ds(0, ROWS_HALF)], core_ss)
    pend["core"] = bulk(crecv.at[pl.ds(0, ROWS_HALF)], core_rs)
    pend.pop("core")()
    acc[:ROWS_PAD, :] = (awh[core] + crecv[...]).astype(BF16)
    for d in PLANE:
        px, py = plane(d)
        pltpu.make_async_remote_copy(
            acc.at[pl.ds(pl.multiple_of((px * 4 + py) * PIECE, PIECE), PIECE)],
            xrecv.at[d], xy_ss, xy_rs,
            device_id=at(px, py, z, core), device_id_type=MESH,
        ).start()
    pend["xy_s"] = bulk(xrecv.at[pl.ds(1, 15)], xy_ss)
    pend["xy"] = bulk(xrecv.at[pl.ds(1, 15)], xy_rs)
    lax.fori_loop(1, TR + 1, lambda i, c: (shift_rows(i), c)[1], 0)

    level = jnp.full((1, TC), noise_ref[0], jnp.int32).astype(F32) / (NOISE_LEVELS - 1)
    sigma = jnp.exp(math.log(2.0) + level * (math.log(0.05) - math.log(2.0)))
    scale = 1.0 / jnp.sqrt(sigma * sigma + 0.25)

    def back_step(n, carry):
        back = jnp.zeros((CPAD, 2 * TC), F32)
        for a in range(3):
            start = pl.multiple_of((2 * n + 2 - a) * TC, TC)
            back = back + lax.dot_general(
                wcat[a], dzc[pl.ds(start, 2 * TC), :], (((1,), (1,)), ((), ())),
                preferred_element_type=F32,
            )
        for half in range(2):
            part = back[:, half * TC : (half + 1) * TC]
            bk32[2 * n + half, :CPAD, :] = part
            d32[pl.ds(2 * n + half, CR, stride=TR), :] = part[:CR] * scale
        return carry

    lax.fori_loop(1, TR // 2 - 1, back_step, 0)

    pend.pop("xy")()
    piece = acc[pl.ds(pl.multiple_of(q * PIECE, PIECE), PIECE), :].astype(F32)
    for d in range(1, 16):
        piece = piece + xrecv[d].astype(F32)
    zbuf[z] = piece.astype(BF16)

    for d in ZLINE:
        pltpu.make_async_remote_copy(
            zbuf.at[z], zbuf.at[z], z_ss, z_rs, device_id=z_dev(d), device_id_type=MESH
        ).start()
    pend["z_s"] = bulk(zbuf.at[pl.ds(0, 7)], z_ss)
    pend["z"] = bulk(zbuf.at[pl.ds(0, 7)], z_rs)

    pend.pop(("halo", 2))()
    pend.pop(("halo", 3))()
    p32[0, TOP : TOP + TC, :] = p32[0, TOP : TOP + TC, :] * up
    p32[TR + 1, TOP : TOP + TC, :] = p32[TR + 1, TOP : TOP + TC, :] * down
    p32[0, TOP - 1 : TOP, :] = corner[0, 0, 7:8, :] * (up * left)
    p32[0, TOP + TC : TOP + TC + 1, :] = corner[0, 1, 0:1, :] * (up * right)
    p32[TR + 1, TOP - 1 : TOP, :] = corner[1, 0, 7:8, :] * (down * left)
    p32[TR + 1, TOP + TC : TOP + TC + 1, :] = corner[1, 1, 0:1, :] * (down * right)
    shift_rows(0)
    shift_rows(TR + 1)

    back_step(0, 0)
    back_step(TR // 2 - 1, 0)

    pend.pop(5)()
    home = (reg * 4 + glob) * 2
    wanted = [(home + step + NGB) % NGB for step in (-1, 0, 1, 2, NGB // 2)]
    for i in range(TR):
        cond = bk32[i, CR : CR + BLK, :].astype(BF16).astype(F32)
        target = targets_ref[0, i]
        for n in range(5):
            mask = (target == wanted[n]).astype(F32)
            cmask[n * BLK : (n + 1) * BLK, i * TC : (i + 1) * TC] = (cond * mask).astype(BF16)
    pend.pop(4)()
    glob_out[...] = jnp.dot(
        cmask[...], interp_v[...].reshape(TR * TC, TC), preferred_element_type=F32
    ).reshape(5, BLK, TC)
    for n, (block, step) in enumerate(((0, -1), (3, 1), (4, 64))):
        pltpu.make_async_remote_copy(
            glob_out.at[block], glob_recv.at[n], gl_ss.at[0], gl_rs.at[0],
            device_id=flat_dev(step), device_id_type=MESH,
        ).start()
    pend["glob_s"] = bulk(glob_recv, gl_ss.at[0])
    pend["glob"] = bulk(glob_recv, gl_rs.at[0])
    pend.pop("z")()
    full = zbuf[0].astype(F32)
    for n in range(1, 8):
        full = full + zbuf[n].astype(F32)
    gbuf[core, q] = (full * SCALE_NORM).astype(BF16)

    for d in PLANE:
        pltpu.make_async_remote_copy(
            gbuf.at[core, q], gbuf.at[core, q], ag_ss, ag_rs.at[d // 4],
            device_id=plane_dev(d), device_id_type=MESH,
        ).start()
    pend["ag_s"] = bulk(gbuf.at[0, pl.ds(0, 15)], ag_ss)

    def igrad_step(n, carry):
        rows = d32[pl.ds(pl.multiple_of(n * 9 * TR, 16), 9 * TR), :]
        ig_v[pl.ds(n * 9, 9)] = rows.reshape(9, TR, TC).astype(BF16)
        return carry

    lax.fori_loop(0, CR // 9, igrad_step, 0)
    pend.pop("glob")()
    own[0] = glob_out[1] + glob_recv[1] + glob_recv[2]
    own[1] = glob_out[2] + glob_recv[0]
    cpl_copy = pltpu.make_async_remote_copy(
        own, cplrecv, gl_ss.at[1], gl_rs.at[1], device_id=other, device_id_type=MESH
    )
    cpl_copy.start()
    pend["cpl_s"] = cpl_copy.wait_send
    pend["cpl"] = cpl_copy.wait_recv

    for dx in (0, 1, 3, 2):
        count = 3 if dx == 0 else 4
        bulk(gbuf.at[0, pl.ds(0, count)], ag_rs.at[dx])()
        column = gbuf.at[core, pl.ds(lax.rem(x + 4 - dx, 4) * 4, 4)]
        pltpu.make_async_remote_copy(
            column, column, fw_ss, fw_rs, device_id=sibling, device_id_type=MESH
        ).start()
    pend["fw_s"] = bulk(gbuf.at[0], fw_ss)
    pend.pop("cpl")()
    ggrad_ref[...] = own[...] + cplrecv[...]
    bulk(gbuf.at[0], fw_rs)()
    for wait in pend.values():
        wait()


def finish(ig_v, gbuf, gg_v, igrad_hbm, wgrad_hbm, bgrad_hbm, ggrad_hbm, w32, b32, g32, sem):
    first = pltpu.make_async_copy(ig_v, igrad_hbm.at[0], sem.at[0])
    first.start()
    for n in range(2):
        g32[:, n : n + 1, :] = gg_v[n, :CG, :].reshape(CG, 1, TC)
    second = pltpu.make_async_copy(g32, ggrad_hbm, sem.at[1])
    second.start()
    for h in range(2):
        for p in range(16):
            part = gbuf[h, p].astype(F32)
            for s in range(PIECE // 8):
                row = p * PIECE + s * 8
                if row >= ROWS_HALF:
                    continue
                k, c = row // HALF, row % HALF + h * HALF
                keep = min(8, CIN - c)
                w32[k, c : c + keep, :] = part[s * 8 : s * 8 + keep]
                if h == 1 and k == 0 and c <= CIN < c + 8:
                    b32[...] = part[s * 8 + CIN - c]

    third = pltpu.make_async_copy(w32, wgrad_hbm, sem.at[2])
    third.start()
    fourth = pltpu.make_async_copy(b32, bgrad_hbm, sem.at[3])
    fourth.start()
    for copy in (first, second, third, fourth):
        copy.wait()


def body(saved_input, pre_act, cotangent, conv_weight, interp, targets, noise_index):
    vmem = pl.BlockSpec(memory_space=pltpu.VMEM)
    smem = pl.BlockSpec(memory_space=pltpu.SMEM)
    hbm = pl.BlockSpec(memory_space=pltpu.HBM)
    dma = pltpu.SemaphoreType.DMA
    pinned = [
        pltpu.with_memory_space_constraint(v, pltpu.HBM)
        for v in (saved_input, pre_act, cotangent, conv_weight, interp, targets)
    ]
    parts = pl.pallas_call(
        kernel,
        out_shape=(
            jax.ShapeDtypeStruct((CR, TR, TC), BF16),
            jax.ShapeDtypeStruct((2, 16, PIECE, CH), BF16),
            jax.ShapeDtypeStruct((2, BLK, TC), F32),
        ),
        in_specs=[hbm] * 6 + [smem],
        out_specs=(vmem, vmem, vmem),
        scratch_shapes=[
            pltpu.VMEM((CIN, TR, TC), BF16),
            pltpu.VMEM((CH, TR, TC), BF16),
            pltpu.VMEM((CH, TR, TC), BF16),
            pltpu.VMEM((9, CIN, CH), BF16),
            pltpu.VMEM((TR, TC, TC), BF16),
            pltpu.SMEM((1, TR), jnp.int32),
            pltpu.VMEM((CH * TR, TC), F32),
            pltpu.VMEM((CPAD * TR, TC), F32),
            pltpu.VMEM((TR + 2, PITCH, CH), F32),
            pltpu.VMEM(((TR + 2) * TC, 3 * CH), BF16),
            pltpu.VMEM((CPAD, TR * TC), BF16),
            pltpu.VMEM((3, CPAD, 3 * CH), BF16),
            pltpu.VMEM((2, TR, CH), F32),
            pltpu.VMEM((2, TR, CH), F32),
            pltpu.VMEM((2, 2, 8, CH), F32),
            pltpu.VMEM((2, CPAD, TC), BF16),
            pltpu.VMEM((3, CPAD, 2 * TC), BF16),
            pltpu.VMEM((TR * TC, TC), BF16),
            pltpu.VMEM((2, 24, CH), F32),
            pltpu.VMEM((3, 2 * TC, 3 * CH), BF16),
            pltpu.VMEM((2, ROWS_PAD, CH), F32),
            pltpu.VMEM((ROWS_PAD, CH), F32),
            pltpu.VMEM((ROWS_ALL, CH), BF16),
            pltpu.VMEM((16, PIECE, CH), BF16),
            pltpu.VMEM((8, PIECE, CH), BF16),
            pltpu.VMEM((TR, CPAD + 8, TC), F32),
            pltpu.VMEM((5 * BLK, TR * TC), BF16),
            pltpu.VMEM((5, BLK, TC), F32),
            pltpu.VMEM((3, BLK, TC), F32),
            pltpu.VMEM((2, BLK, TC), F32),
            pltpu.VMEM((2, BLK, TC), F32),
            dma((6,)),
            dma((4,)),
            dma((4,)),
            dma,
            dma,
            dma,
            dma,
            dma,
            dma,
            dma,
            dma((4,)),
            dma,
            dma,
            dma((2,)),
            dma((2,)),
        ],
        compiler_params=pltpu.CompilerParams(
            collective_id=0, has_side_effects=True, vmem_limit_bytes=40 << 20
        ),
        cost_estimate=pl.CostEstimate(
            flops=2 * 2 * CIN * 9 * CH * TR * TC, bytes_accessed=4 << 20, transcendentals=CH * TR * TC
        ),
    )(*pinned, noise_index)
    igrad, wgrad, bgrad, ggrad = pl.pallas_call(
        finish,
        out_shape=(
            pltpu.HBM((1, CR, TR, TC), BF16),
            pltpu.HBM((9, CIN, CH), F32),
            pltpu.HBM((CH,), F32),
            pltpu.HBM((CG, 2, TC), F32),
        ),
        in_specs=[vmem] * 3,
        out_specs=(hbm, hbm, hbm, hbm),
        scratch_shapes=[
            pltpu.VMEM((9, CIN, CH), F32),
            pltpu.VMEM((CH,), F32),
            pltpu.VMEM((CG, 2, TC), F32),
            dma((4,)),
        ],
        compiler_params=pltpu.CompilerParams(vmem_limit_bytes=16 << 20),
    )(*parts)
    return igrad, wgrad, bgrad, jnp.transpose(ggrad, (1, 0, 2))


def solution(mesh):
    in_specs = (
        P("cpl", None, "reg", "glob"),
        P("cpl", None, "reg", "glob"),
        P("cpl", None, "reg", "glob"),
        P(),
        P("glob", "reg", None, None),
        P("glob", "reg"),
        P("cpl"),
    )
    out_specs = (P("cpl", None, "reg", "glob"), P(), P(), P(("reg", "glob"), None, None))
    return jax.shard_map(body, mesh=mesh, in_specs=in_specs, out_specs=out_specs, check_vma=False)
```
